32 devices in a mesh: section: 8 (over z, y), rep: 4 (over x, core).
Axes of the slice: x: 2, y: 2, z: 4, core: 2. Of those that a mesh axis runs over, the one named last changes fastest.
Arguments:
- features: bfloat16 [4096, 256], P(('section', 'rep')), may hold values from -6 to 6
- tiles: bfloat16 [32, 64, 128, 128], P(('section', 'rep')), may hold values from 0 to 0.019042969
- columns: int32 [32, 64], P(('section', 'rep')), may hold values from 0 to 31
- weight: bfloat16 [256, 256], replicated, may hold values from -0.375 to 0.375
Outputs:
- hidden: bfloat16 [4096, 256], P(('section', 'rep'))
The draws below stay inside these ranges and needn't reach their ends.
All inputs are finite; a program needn't handle non-finite values.
Results may differ from the reference program's by a relative error of at most 0.0049.
Values may be sent and summed in bfloat16 or wider, within the bound.
A program may use at most 64 MiB of HBM per device.

```python
import math
import jax
import jax.numpy as jnp
import numpy as np
from jax import lax

F = 256
BLK = 128
K = 64
NODES = 4096
NB = 32


def plant(array, stream_key, smallest, largest):
    spot = [jax.random.randint(jax.random.fold_in(stream_key, axis), (), 0, length) for axis, length in enumerate(array.shape)]
    longest = array.shape.index(max(array.shape))
    beside = spot[:longest] + [(spot[longest] + 1) % array.shape[longest]] + spot[longest + 1:]
    return array.at[tuple(spot)].set(smallest).at[tuple(beside)].set(largest)


def shard_levels(key, extent, shards, least, largest):
    def one(dim, parts):
        draws = jax.random.uniform(jax.random.fold_in(jax.random.fold_in(key, 6), dim), (parts,), jnp.float32, least / len(shards), largest / len(shards))
        return jnp.repeat(jnp.exp(draws), extent[dim] // parts).reshape((-1,) + (1,) * (len(extent) - dim - 1))

    level = one(*shards[0])
    for cut in shards[1:]:
        level = level * one(*cut)
    return level


def rank_table(number_of, skew):
    portions = [(1 << 20) // math.isqrt(rank ** skew) + 1 for rank in range(1, number_of + 1)]
    scale = 1 + sum(portions) // (1 << 30)
    return np.cumsum(np.array([max(1, weight // scale) for weight in portions]))


def ranked_ids(rng, dims, amount, slope):
    table = rank_table(amount, slope)
    lot = jax.random.randint(jax.random.fold_in(rng, 1), dims, 0, int(table[amount - 1]))
    rank = jnp.searchsorted(jnp.asarray(table, jnp.int32), lot, side="right")
    return jax.random.permutation(jax.random.fold_in(rng, 2), amount)[rank].astype(jnp.int32)


def normal_values(key, dims, scale, bound, pieces=(), kind=jnp.bfloat16):
    loudness = shard_levels(key, dims, pieces, -0.22, 0.18) if pieces else 1.0
    entries = jax.random.normal(key, dims, jnp.float32) * scale * loudness
    return jnp.minimum(jnp.maximum(entries, -bound), bound).astype(kind)


def setup_inputs(seed: int = 0) -> dict:
    streams_of = jax.random.split(jax.random.key(seed), 5)
    return {
        "features": normal_values(streams_of[0], (NODES, F), 1.0, 6.0, ((0, 32),)),
        "tiles": jnp.clip(0.019042969 * jax.random.uniform(streams_of[1], (NB, K, BLK, BLK), jnp.float32) ** shard_levels(streams_of[1], (NB, K, BLK, BLK), ((0, 32),), -0.2, 0.2), 0.0, 0.019042969).astype(jnp.bfloat16),
        "columns": plant(ranked_ids(streams_of[2], (NB, K), NB, 1), jax.random.fold_in(streams_of[2], 3), 0, NB - 1).astype(jnp.int32),
        "weight": normal_values(streams_of[3], (F, F), F ** -0.5, 0.375),
    }


def reference(features, tiles, columns, weight):
    blocks = features.reshape(NB, BLK, F)

    def one_block(pair):
        tile_rows, cols = pair
        picked = blocks[cols]
        summed = jnp.einsum("kij,kjf->if", tile_rows.astype(jnp.float32), picked.astype(jnp.float32))
        return summed.astype(jnp.bfloat16)

    aggregated = lax.map(one_block, (tiles, columns)).reshape(NODES, F)
    product = jnp.dot(aggregated, weight, preferred_element_type=jnp.float32)
    return jnp.maximum(product, 0.0).astype(jnp.bfloat16)
```

```python
import functools
import jax
import jax.numpy as jnp
from jax import lax
from jax.experimental import pallas as pl
from jax.experimental.pallas import tpu as pltpu
from jax.sharding import PartitionSpec as P

GROUP = 8


def flip(index, mask):
    bit = 1
    while bit <= mask:
        if mask & bit:
            index = index + bit - 2 * bit * ((index // bit) % 2)
        bit *= 2
    return index


def arrivals(columns, across):
    keys = []
    for m in range(columns):
        if m:
            keys.append(("column", m))
        keys.append(("beside", m))
        keys.append(("sibling", m, 0, 0))
        keys.append(("sibling", m, 1, 0))
        for q in range(1, across):
            keys.append(("across", m, q))
            keys.append(("diagonal", m, q, 0))
            keys.append(("diagonal", m, q, 1))
            keys.append(("sibling", m, 0, q))
            keys.append(("sibling diagonal", m, q, 0))
            keys.append(("sibling diagonal", m, q, 1))
    return {key: spot for spot, key in enumerate(keys)}


def kernel(columns, across, col_ref, f_ref, t_ref, w_ref, out_ref, blocks, tiles, weight, send_sems, recv_sems, local_sems):
    rep = 2 * across
    side = blocks.shape[1]
    half = side // 2
    section_at = lax.axis_index("section")
    rep_at = lax.axis_index("rep")
    a, b = section_at // 2, section_at % 2
    x, c = rep_at // 2, rep_at % 2
    spots = arrivals(columns, across)
    sent = []

    def device(m, beside, q, other):
        return flip(a, m) * 2 + flip(b, beside), flip(x, q) * 2 + flip(c, other)

    def block(m, beside, q, other=0):
        s, r = device(m, beside, q, other)
        return blocks.at[s * rep + r]

    def part(ref, h):
        return ref.at[pl.ds(h * half, half)]

    def send(src, dst, to, key):
        copy = pltpu.make_async_remote_copy(
            src_ref=src, dst_ref=dst, send_sem=send_sems.at[len(sent)], recv_sem=recv_sems.at[spots[key]],
            device_id=to, device_id_type=pl.DeviceIdType.MESH)
        copy.start()
        sent.append(copy)

    def arrive(dst, key):
        pltpu.make_async_remote_copy(
            src_ref=dst, dst_ref=dst, send_sem=send_sems.at[0], recv_sem=recv_sems.at[spots[key]],
            device_id=device(0, 0, 0, 1), device_id_type=pl.DeviceIdType.MESH).wait_recv()

    partners = [device(m, 0, 0, 0) for m in range(1, columns)]
    partners += [device(0, 0, q, 0) for q in range(1, across)]
    partners += [device(0, 1, 0, 0), device(0, 0, 0, 1)]
    barrier = pltpu.get_barrier_semaphore()
    for partner in partners:
        pl.semaphore_signal(barrier, inc=1, device_id=partner, device_id_type=pl.DeviceIdType.MESH)
    pl.semaphore_wait(barrier, len(partners))

    sibling = device(0, 0, 0, 1)
    beside = device(0, 1, 0, 0)

    def spread(src, m):
        for q in range(1, across):
            send(src, block(m, 0, 0), device(0, 0, q, 0), ("across", m, q))
        send(src, block(m, 0, 0), beside, ("beside", m))
        send(src, block(m, 0, 0), sibling, ("sibling", m, 0, 0))

    for m in range(1, columns):
        send(f_ref, block(0, 0, 0), device(m, 0, 0, 0), ("column", m))
    spread(f_ref, 0)
    own = pltpu.make_async_copy(f_ref, block(0, 0, 0), local_sems.at[0])
    load_tiles = pltpu.make_async_copy(t_ref, tiles, local_sems.at[1])
    load_weight = pltpu.make_async_copy(w_ref, weight, local_sems.at[2])
    own.start()
    load_tiles.start()
    load_weight.start()

    def relay(m):
        for q in range(1, across):
            got = block(m, 0, q)
            arrive(got, ("across", m, q))
            send(part(got, 0), part(got, 0), beside, ("diagonal", m, q, 0))
            send(got, got, sibling, ("sibling", m, 0, q))
        got = block(m, 1, 0)
        arrive(got, ("beside", m))
        for q in range(1, across):
            send(part(got, 1), part(got, 1), device(0, 0, q, 0), ("diagonal", m, q, 1))
        send(got, got, sibling, ("sibling", m, 1, 0))

    def diagonal(m):
        for q in range(1, across):
            for h in range(2):
                got = part(block(m, 1, q), h)
                arrive(got, ("diagonal", m, q, h))
                send(got, got, sibling, ("sibling diagonal", m, q, h))

    for m in range(1, columns):
        got = block(m, 0, 0)
        arrive(got, ("column", m))
        spread(got, m)
        relay(m - 1)
        if m > 1:
            diagonal(m - 2)
    relay(columns - 1)
    if columns > 1:
        diagonal(columns - 2)
    diagonal(columns - 1)

    for m in range(columns):
        arrive(block(m, 0, 0, 1), ("sibling", m, 0, 0))
        arrive(block(m, 1, 0, 1), ("sibling", m, 1, 0))
        for q in range(1, across):
            arrive(block(m, 0, q, 1), ("sibling", m, 0, q))
            for h in range(2):
                arrive(part(block(m, 1, q, 1), h), ("sibling diagonal", m, q, h))
    own.wait()
    load_tiles.wait()
    load_weight.wait()

    number = tiles.shape[1]
    group = GROUP if number % GROUP == 0 else 1

    def step(i, total):
        left = jnp.concatenate([tiles[0, i * group + g] for g in range(group)], axis=1)
        right = jnp.concatenate([blocks[col_ref[0, i * group + g]] for g in range(group)], axis=0)
        return total + jnp.dot(left, right, preferred_element_type=jnp.float32)

    total = lax.fori_loop(0, number // group, step, jnp.zeros(out_ref.shape, jnp.float32), unroll=True)
    aggregated = total.astype(jnp.bfloat16)
    product = jnp.dot(aggregated, weight[...], preferred_element_type=jnp.float32)
    out_ref[...] = jnp.maximum(product, 0.0).astype(out_ref.dtype)
    for copy in sent:
        copy.wait_send()


def on_device(sections, reps, features, tiles, columns, weight):
    along, across = sections // 2, reps // 2
    side, width = features.shape
    arriving = len(arrivals(along, across))
    return pl.pallas_call(
        functools.partial(kernel, along, across),
        out_shape=jax.ShapeDtypeStruct((side, weight.shape[1]), jnp.bfloat16),
        in_specs=[pl.BlockSpec(memory_space=pltpu.SMEM)] + [pl.BlockSpec(memory_space=pl.ANY)] * 3,
        out_specs=pl.BlockSpec(memory_space=pltpu.VMEM),
        scratch_shapes=[
            pltpu.VMEM((sections * reps, side, width), features.dtype),
            pltpu.VMEM(tiles.shape, tiles.dtype),
            pltpu.VMEM(weight.shape, weight.dtype),
            pltpu.SemaphoreType.DMA((arriving,)),
            pltpu.SemaphoreType.DMA((arriving,)),
            pltpu.SemaphoreType.DMA((3,)),
        ],
        compiler_params=pltpu.CompilerParams(
            collective_id=0, has_side_effects=True, vmem_limit_bytes=56 * 1024 * 1024),
        cost_estimate=pl.CostEstimate(
            flops=2 * tiles.size * width, bytes_accessed=2 * (tiles.size + features.size * sections * reps),
            transcendentals=0),
    )(columns, features, tiles, weight)


def solution(mesh):
    return jax.shard_map(
        functools.partial(on_device, mesh.shape["section"], mesh.shape["rep"]),
        mesh=mesh,
        in_specs=(
            P(("section", "rep"), None),
            P(("section", "rep"), None, None, None),
            P(("section", "rep"), None),
            P(),
        ),
        out_specs=P(("section", "rep"), None),
        check_vma=False,
    )
```

```python
import functools
import jax
import jax.numpy as jnp
from jax import lax
from jax.experimental import pallas as pl
from jax.experimental.pallas import tpu as pltpu
from jax.sharding import PartitionSpec as P

GROUP = 8

def flip(index, wanted):
    return index + wanted - 2 * wanted * (index % 2)

def steps_of(columns):
    return [(0, 0)] + [(side, s) for s in range(1, columns) for side in (-1, 1)]

def arrivals(columns, across):
    keys = []
    for item in steps_of(columns):
        if item[1]:
            keys.append(("column", item))
        keys.append(("beside", item))
        keys.append(("sibling", item, 0, 0))
        keys.append(("sibling", item, 1, 0))
        for q in range(1, across):
            keys.append(("across", item, q))
            keys.append(("diagonal", item, q, 0))
            keys.append(("diagonal", item, q, 1))
            keys.append(("sibling", item, 0, q))
            keys.append(("sibling diagonal", item, q, 0))
            keys.append(("sibling diagonal", item, q, 1))
    return {key: spot for spot, key in enumerate(keys)}

def kernel(columns, across, col_ref, f_ref, t_ref, w_ref, out_ref, blocks, tiles, weight, send_sems, recv_sems, local_sems):
    rep = 2 * across
    side_rows = blocks.shape[1]
    half = side_rows // 2
    section_at = lax.axis_index("section")
    rep_at = lax.axis_index("rep")
    a, b = section_at // 2, section_at % 2
    x, c = rep_at // 2, rep_at % 2
    spots = arrivals(columns, across)
    sent = []

    def device(item, beside, q, other):
        at = lax.rem(x + q, across) if q else x
        return (a + item[0] * item[1]) * 2 + flip(b, beside), at * 2 + flip(c, other)

    here = (0, 0)

    def block(item, beside, q, other=0):
        s, r = device(item, beside, q, other)
        return blocks.at[s * rep + r]

    def part(ref, h):
        return ref.at[pl.ds(h * half, half)]

    def there(item):
        if item[1] == 0:
            return None
        return a >= item[1] if item[0] < 0 else a + item[1] < columns

    def both(item, condition):
        known = there(item)
        return condition if known is None else known & condition

    def only(condition, work):
        if condition is None:
            work()
        else:
            pl.when(condition)(work)

    def send(src, dst, to, key, condition):
        copy = pltpu.make_async_remote_copy(
            src_ref=src, dst_ref=dst, send_sem=send_sems.at[spots[key]], recv_sem=recv_sems.at[spots[key]],
            device_id=to, device_id_type=pl.DeviceIdType.MESH)
        copy.start()
        sent.append((src.shape[0], key, condition))

    def arrive(dst, key):
        pltpu.make_async_remote_copy(
            src_ref=dst, dst_ref=dst, send_sem=send_sems.at[0], recv_sem=recv_sems.at[spots[key]],
            device_id=device(here, 0, 0, 1), device_id_type=pl.DeviceIdType.MESH).wait_recv()

    below, above = device((-1, 1), 0, 0, 0), device((1, 1), 0, 0, 0)
    has_below, has_above = a >= 1, a + 1 < columns
    sibling = device(here, 0, 0, 1)
    beside = device(here, 1, 0, 0)

    barrier = pltpu.get_barrier_semaphore()

    def greet(partner):
        pl.semaphore_signal(barrier, inc=1, device_id=partner, device_id_type=pl.DeviceIdType.MESH)

    partners = [device(here, 0, q, 0) for q in range(1, across)] + [beside, sibling]
    for partner in partners:
        greet(partner)
    only(has_below, lambda: greet(below))
    only(has_above, lambda: greet(above))
    pl.semaphore_wait(barrier, len(partners) + jnp.where(has_below, 1, 0) + jnp.where(has_above, 1, 0))

    def pass_on(src, item):
        s = item[1] + 1
        dst = block(item, 0, 0)
        if item[0] <= 0 and s < columns:
            only(has_above, lambda: send(src, dst, above, ("column", (-1, s)), lambda: both(item, has_above)))
        if item[0] >= 0 and s < columns:
            only(has_below, lambda: send(src, dst, below, ("column", (1, s)), lambda: both(item, has_below)))

    def spread(src, item):
        dst = block(item, 0, 0)
        for q in range(1, across):
            send(src, dst, device(here, 0, q, 0), ("across", item, q), lambda: there(item))
        send(src, dst, beside, ("beside", item), lambda: there(item))
        send(src, dst, sibling, ("sibling", item, 0, 0), lambda: there(item))

    def receive(item):
        got = block(item, 0, 0)
        arrive(got, ("column", item))
        pass_on(got, item)
        spread(got, item)

    def relay(item):
        for q in range(1, across):
            got = block(item, 0, across - q)
            arrive(got, ("across", item, q))
            send(part(got, 0), part(got, 0), beside, ("diagonal", item, q, 0), lambda: there(item))
            send(got, got, sibling, ("sibling", item, 0, q), lambda: there(item))
        got = block(item, 1, 0)
        arrive(got, ("beside", item))
        for q in range(1, across):
            send(part(got, 1), part(got, 1), device(here, 0, q, 0), ("diagonal", item, q, 1), lambda: there(item))
        send(got, got, sibling, ("sibling", item, 1, 0), lambda: there(item))

    def diagonal(item):
        for q in range(1, across):
            for h in range(2):
                got = part(block(item, 1, across - q), h)
                arrive(got, ("diagonal", item, q, h))
                send(got, got, sibling, ("sibling diagonal", item, q, h), lambda: there(item))

    def from_sibling(item):
        arrive(block(item, 0, 0, 1), ("sibling", item, 0, 0))
        arrive(block(item, 1, 0, 1), ("sibling", item, 1, 0))
        for q in range(1, across):
            arrive(block(item, 0, across - q, 1), ("sibling", item, 0, q))
            for h in range(2):
                arrive(part(block(item, 1, across - q, 1), h), ("sibling diagonal", item, q, h))

    pass_on(f_ref, here)
    spread(f_ref, here)
    own = pltpu.make_async_copy(f_ref, block(here, 0, 0), local_sems.at[0])
    load_tiles = pltpu.make_async_copy(t_ref, tiles, local_sems.at[1])
    load_weight = pltpu.make_async_copy(w_ref, weight, local_sems.at[2])
    own.start()
    load_tiles.start()
    load_weight.start()

    rounds = [[here]] + [[(-1, s), (1, s)] for s in range(1, columns)]
    for s in range(len(rounds) + 2):
        for stage, at in ((receive, s), (relay, s - 1), (diagonal, s - 2)):
            if 0 <= at < len(rounds) and not (stage is receive and at == 0):
                for item in rounds[at]:
                    only(there(item), functools.partial(stage, item))
    for items in rounds:
        for item in items:
            only(there(item), functools.partial(from_sibling, item))
    own.wait()
    load_tiles.wait()
    load_weight.wait()

    number = tiles.shape[1]
    group = GROUP if number % GROUP == 0 else 1

    def step(i, total):
        left = jnp.concatenate([tiles[0, i * group + g] for g in range(group)], axis=1)
        right = jnp.concatenate([blocks[col_ref[0, i * group + g]] for g in range(group)], axis=0)
        return total + jnp.dot(left, right, preferred_element_type=jnp.float32)

    total = lax.fori_loop(0, number // group, step, jnp.zeros(out_ref.shape, jnp.float32), unroll=True)
    aggregated = total.astype(jnp.bfloat16)
    product = jnp.dot(aggregated, weight[...], preferred_element_type=jnp.float32)
    out_ref[...] = jnp.maximum(product, 0.0).astype(out_ref.dtype)

    def gone(rows, key):
        src = blocks.at[0, pl.ds(0, rows)]
        pltpu.make_async_remote_copy(
            src_ref=src, dst_ref=src, send_sem=send_sems.at[spots[key]], recv_sem=recv_sems.at[spots[key]],
            device_id=sibling, device_id_type=pl.DeviceIdType.MESH).wait_send()

    for rows, key, condition in sent:
        only(condition(), functools.partial(gone, rows, key))

def on_device(sections, reps, features, tiles, columns, weight):
    along, across = sections // 2, reps // 2
    side, width = features.shape
    arriving = len(arrivals(along, across))

    return pl.pallas_call(
        functools.partial(kernel, along, across),
        out_shape=jax.ShapeDtypeStruct((side, weight.shape[1]), jnp.bfloat16),
        in_specs=[pl.BlockSpec(memory_space=pltpu.SMEM)] + [pl.BlockSpec(memory_space=pltpu.HBM)] * 3,
        out_specs=pl.BlockSpec(memory_space=pltpu.VMEM),
        scratch_shapes=[
            pltpu.VMEM((sections * reps, side, width), features.dtype),
            pltpu.VMEM(tiles.shape, tiles.dtype),
            pltpu.VMEM(weight.shape, weight.dtype),
            pltpu.SemaphoreType.DMA((arriving,)),
            pltpu.SemaphoreType.DMA((arriving,)),
            pltpu.SemaphoreType.DMA((3,)),
        ],
        compiler_params=pltpu.CompilerParams(
            collective_id=0, has_side_effects=True, vmem_limit_bytes=56 * 1024 * 1024),
        cost_estimate=pl.CostEstimate(
            flops=2 * tiles.size * width, bytes_accessed=2 * (tiles.size + features.size * sections * reps),
            transcendentals=0),
    )(columns, features, tiles, weight)

def solution(mesh):
    return jax.shard_map(
        functools.partial(on_device, mesh.shape["section"], mesh.shape["rep"]),
        mesh=mesh,
        in_specs=(
            P(("section", "rep"), None),
            P(("section", "rep"), None, None, None),
            P(("section", "rep"), None),
            P(),
        ),
        out_specs=P(("section", "rep"), None),
        check_vma=False,
    )
```

```python
import functools
import jax
import jax.numpy as jnp
from jax import lax
from jax.experimental import pallas as pl
from jax.experimental.pallas import tpu as pltpu
from jax.sharding import PartitionSpec as P

GROUP = 8


def flip(index, mask):
    bit = 1
    while bit <= mask:
        if mask & bit:
            index = index + bit - 2 * bit * ((index // bit) % 2)
        bit *= 2
    return index


def arrivals(columns, across):
    keys = []
    for m in range(columns):
        if m:
            keys.append(("column", m))
        keys.append(("beside", m))
        keys.append(("sibling", m, 0, 0))
        keys.append(("sibling", m, 1, 0))
        for q in range(1, across):
            keys.append(("across", m, q))
            keys.append(("diagonal", m, q, 0))
            keys.append(("diagonal", m, q, 1))
            keys.append(("sibling", m, 0, q))
            keys.append(("sibling diagonal", m, q, 0))
            keys.append(("sibling diagonal", m, q, 1))
    return {key: spot for spot, key in enumerate(keys)}


def kernel(columns, across, col_ref, f_ref, t_ref, w_ref, out_ref, blocks, tiles, weight, send_sems, recv_sems, local_sems):
    rep = 2 * across
    side = blocks.shape[1]
    half = side // 2
    section_at = lax.axis_index("section")
    rep_at = lax.axis_index("rep")
    a, b = section_at // 2, section_at % 2
    x, c = rep_at // 2, rep_at % 2
    spots = arrivals(columns, across)
    sent = []

    def device(m, beside, q, other):
        return flip(a, m) * 2 + flip(b, beside), flip(x, q) * 2 + flip(c, other)

    def block(m, beside, q, other=0):
        s, r = device(m, beside, q, other)
        return blocks.at[s * rep + r]

    def part(ref, h):
        return ref.at[pl.ds(h * half, half)]

    def send(src, dst, to, key):
        copy = pltpu.make_async_remote_copy(
            src_ref=src, dst_ref=dst, send_sem=send_sems.at[len(sent)], recv_sem=recv_sems.at[spots[key]],
            device_id=to, device_id_type=pl.DeviceIdType.MESH)
        copy.start()
        sent.append(copy)

    def arrive(dst, key):
        pltpu.make_async_remote_copy(
            src_ref=dst, dst_ref=dst, send_sem=send_sems.at[0], recv_sem=recv_sems.at[spots[key]],
            device_id=device(0, 0, 0, 1), device_id_type=pl.DeviceIdType.MESH).wait_recv()

    partners = [device(m, 0, 0, 0) for m in range(1, columns)]
    partners += [device(0, 0, q, 0) for q in range(1, across)]
    partners += [device(0, 1, 0, 0), device(0, 0, 0, 1)]
    barrier = pltpu.get_barrier_semaphore()
    for partner in partners:
        pl.semaphore_signal(barrier, inc=1, device_id=partner, device_id_type=pl.DeviceIdType.MESH)
    pl.semaphore_wait(barrier, len(partners))

    sibling = device(0, 0, 0, 1)
    beside = device(0, 1, 0, 0)

    def spread(src, m):
        if m != 1:
            for q in range(1, across):
                send(src, block(m, 0, 0), device(0, 0, q, 0), ("across", m, q))
            send(src, block(m, 0, 0), beside, ("beside", m))
        send(src, block(m, 0, 0), sibling, ("sibling", m, 0, 0))

    def climb(m):
        send(f_ref, block(0, 0, 0), device(m, 0, 0, 0), ("column", m))

    for m in range(2, columns):
        climb(m)
    spread(f_ref, 0)
    if columns > 1:
        climb(1)
    own = pltpu.make_async_copy(f_ref, block(0, 0, 0), local_sems.at[0])
    load_tiles = pltpu.make_async_copy(t_ref, tiles, local_sems.at[1])
    load_weight = pltpu.make_async_copy(w_ref, weight, local_sems.at[2])
    own.start()
    load_tiles.start()
    load_weight.start()

    def relay(m):
        for q in range(1, across):
            got = block(m, 0, q)
            arrive(got, ("across", m, q))
            send(part(got, 0), part(got, 0), beside, ("diagonal", m, q, 0))
            if m == 0 and columns > 1:
                send(got, got, device(1, 0, 0, 0), ("across", 1, q))
            send(got, got, sibling, ("sibling", m, 0, q))
        got = block(m, 1, 0)
        arrive(got, ("beside", m))
        for q in range(1, across):
            send(part(got, 1), part(got, 1), device(0, 0, q, 0), ("diagonal", m, q, 1))
        if m == 0 and columns > 1:
            send(got, got, device(1, 0, 0, 0), ("beside", 1))
        send(got, got, sibling, ("sibling", m, 1, 0))

    def diagonal(m):
        for q in range(1, across):
            for h in range(2):
                got = part(block(m, 1, q), h)
                arrive(got, ("diagonal", m, q, h))
                send(got, got, sibling, ("sibling diagonal", m, q, h))

    def column(m):
        got = block(m, 0, 0)
        arrive(got, ("column", m))
        spread(got, m)

    relay(0)
    late = list(range(2, columns))
    for m in late[:1]:
        column(m)
    diagonal(0)
    if columns > 1:
        column(1)
        relay(1)
    for m in late[1:]:
        column(m)
        relay(m - 1)
    if columns > 1:
        diagonal(1)
    for m in late[:-1]:
        diagonal(m)
    for m in late[-1:]:
        relay(m)
        diagonal(m)

    for m in range(columns):
        arrive(block(m, 0, 0, 1), ("sibling", m, 0, 0))
        arrive(block(m, 1, 0, 1), ("sibling", m, 1, 0))
        for q in range(1, across):
            arrive(block(m, 0, q, 1), ("sibling", m, 0, q))
            for h in range(2):
                arrive(part(block(m, 1, q, 1), h), ("sibling diagonal", m, q, h))
    own.wait()
    load_tiles.wait()
    load_weight.wait()

    number = tiles.shape[1]
    group = GROUP if number % GROUP == 0 else 1

    def step(i, total):
        left = jnp.concatenate([tiles[0, i * group + g] for g in range(group)], axis=1)
        right = jnp.concatenate([blocks[col_ref[0, i * group + g]] for g in range(group)], axis=0)
        return total + jnp.dot(left, right, preferred_element_type=jnp.float32)

    total = lax.fori_loop(0, number // group, step, jnp.zeros(out_ref.shape, jnp.float32), unroll=True)
    aggregated = total.astype(jnp.bfloat16)
    product = jnp.dot(aggregated, weight[...], preferred_element_type=jnp.float32)
    out_ref[...] = jnp.maximum(product, 0.0).astype(out_ref.dtype)
    for copy in sent:
        copy.wait_send()


def on_device(sections, reps, features, tiles, columns, weight):
    along, across = sections // 2, reps // 2
    side, width = features.shape
    arriving = len(arrivals(along, across))
    return pl.pallas_call(
        functools.partial(kernel, along, across),
        out_shape=jax.ShapeDtypeStruct((side, weight.shape[1]), jnp.bfloat16),
        in_specs=[pl.BlockSpec(memory_space=pltpu.SMEM)] + [pl.BlockSpec(memory_space=pl.ANY)] * 3,
        out_specs=pl.BlockSpec(memory_space=pltpu.VMEM),
        scratch_shapes=[
            pltpu.VMEM((sections * reps, side, width), features.dtype),
            pltpu.VMEM(tiles.shape, tiles.dtype),
            pltpu.VMEM(weight.shape, weight.dtype),
            pltpu.SemaphoreType.DMA((arriving,)),
            pltpu.SemaphoreType.DMA((arriving,)),
            pltpu.SemaphoreType.DMA((3,)),
        ],
        compiler_params=pltpu.CompilerParams(
            collective_id=0, has_side_effects=True, vmem_limit_bytes=56 * 1024 * 1024),
        cost_estimate=pl.CostEstimate(
            flops=2 * tiles.size * width, bytes_accessed=2 * (tiles.size + features.size * sections * reps),
            transcendentals=0),
    )(columns, features, tiles, weight)


def solution(mesh):
    return jax.shard_map(
        functools.partial(on_device, mesh.shape["section"], mesh.shape["rep"]),
        mesh=mesh,
        in_specs=(
            P(("section", "rep"), None),
            P(("section", "rep"), None, None, None),
            P(("section", "rep"), None),
            P(),
        ),
        out_specs=P(("section", "rep"), None),
        check_vma=False,
    )
```

```python
import functools
import jax
import jax.numpy as jnp
from jax import lax
from jax.experimental import pallas as pl
from jax.experimental.pallas import tpu as pltpu
from jax.sharding import PartitionSpec as P

GROUP = 8

def flip(index, wanted):
    return index + wanted - 2 * wanted * (index % 2)

def steps_of(columns):
    return [(0, 0)] + [(side, s) for s in range(1, columns) for side in (-1, 1)]

def arrivals(columns, across):
    keys = []
    for item in steps_of(columns):
        if item[1]:
            keys.append(("column", item))
        keys.append(("beside", item))
        keys.append(("sibling", item, 0, 0))
        keys.append(("sibling", item, 1, 0))
        for q in range(1, across):
            keys.append(("across", item, q))
            keys.extend(("diagonal", item, q, h) for h in range(3))
            keys.append(("sibling", item, 0, q))
            keys.extend(("sibling diagonal", item, q, h) for h in range(3))
    return {key: spot for spot, key in enumerate(keys)}

def kernel(columns, across, col_ref, f_ref, t_ref, w_ref, out_ref, blocks, tiles, weight, send_sems, recv_sems, local_sems):
    rep = 2 * across
    side_rows = blocks.shape[1]
    half = side_rows // 2
    section_at = lax.axis_index("section")
    rep_at = lax.axis_index("rep")
    a, b = section_at // 2, section_at % 2
    x, c = rep_at // 2, rep_at % 2
    spots = arrivals(columns, across)
    sent, climbed = [], []

    def device(item, beside, q, other):
        at = lax.rem(x + q, across) if q else x
        return (a + item[0] * item[1]) * 2 + flip(b, beside), at * 2 + flip(c, other)

    here = (0, 0)

    def block(item, beside, q, other=0):
        s, r = device(item, beside, q, other)
        return blocks.at[s * rep + r]

    def direct(item):
        return item[1] in (0, columns - 1)

    def pieces(item):
        return (0,) if direct(item) else (1, 2)

    def part(ref, h):
        if h == 0:
            return ref
        h = h - 1
        return ref.at[pl.ds(h * half, half)]

    def there(item):
        if item[1] == 0:
            return None
        return a >= item[1] if item[0] < 0 else a + item[1] < columns

    def only(condition, work):
        if condition is None:
            work()
        else:
            pl.when(condition)(work)

    def send(src, dst, to, key, condition):
        copy = pltpu.make_async_remote_copy(
            src_ref=src, dst_ref=dst, send_sem=send_sems.at[spots[key]], recv_sem=recv_sems.at[spots[key]],
            device_id=to, device_id_type=pl.DeviceIdType.MESH)
        copy.start()
        if condition is not None:
            sent.append((src.shape[0], key, condition))

    def arrive(dst, key):
        pltpu.make_async_remote_copy(
            src_ref=dst, dst_ref=dst, send_sem=send_sems.at[0], recv_sem=recv_sems.at[spots[key]],
            device_id=device(here, 0, 0, 1), device_id_type=pl.DeviceIdType.MESH).wait_recv()

    def gone(rows, key):
        src = blocks.at[0, pl.ds(0, rows)]
        pltpu.make_async_remote_copy(
            src_ref=src, dst_ref=src, send_sem=send_sems.at[spots[key]], recv_sem=recv_sems.at[spots[key]],
            device_id=device(here, 0, 0, 1), device_id_type=pl.DeviceIdType.MESH).wait_send()

    sibling = device(here, 0, 0, 1)
    beside = device(here, 1, 0, 0)

    barrier = pltpu.get_barrier_semaphore()

    def greet(partner):
        pl.semaphore_signal(barrier, inc=1, device_id=partner, device_id_type=pl.DeviceIdType.MESH)

    partners = [device(here, 0, q, 0) for q in range(1, across)] + [beside, sibling]
    partners += [device(here, 1, q, 0) for q in range(1, across)]
    partners += [(lax.rem(a + d, columns) * 2 + b, rep_at) for d in range(1, columns)]
    for partner in partners:
        greet(partner)
    pl.semaphore_wait(barrier, len(partners))

    def climb(s):
        for side, condition in ((-1, a + s < columns), (1, a >= s)):
            to, key = device((-side, s), 0, 0, 0), ("column", (side, s))
            only(condition, functools.partial(send, f_ref, block(here, 0, 0), to, key, None))
            climbed.append((s, key, condition))

    def wait_climb(s):
        for distance, key, condition in climbed:
            if distance == s:
                only(condition, functools.partial(gone, f_ref.shape[0], key))

    def spread(src, item):
        dst = block(item, 0, 0)
        for q in range(1, across):
            send(src, dst, device(here, 0, q, 0), ("across", item, q), lambda: there(item))
        send(src, dst, beside, ("beside", item), lambda: there(item))
        if direct(item):
            for q in range(1, across):
                send(src, dst, device(here, 1, q, 0), ("diagonal", item, q, 0), lambda: there(item))
        send(src, dst, sibling, ("sibling", item, 0, 0), lambda: there(item))

    def receive(item):
        got = block(item, 0, 0)
        arrive(got, ("column", item))
        spread(got, item)

    def relay(item):
        for q in range(1, across):
            got = block(item, 0, across - q)
            arrive(got, ("across", item, q))
            if not direct(item):
                send(part(got, 1), part(got, 1), beside, ("diagonal", item, q, 1), lambda: there(item))
            send(got, got, sibling, ("sibling", item, 0, q), lambda: there(item))
        got = block(item, 1, 0)
        arrive(got, ("beside", item))
        for q in range(1, across):
            if not direct(item):
                send(part(got, 2), part(got, 2), device(here, 0, q, 0), ("diagonal", item, q, 2), lambda: there(item))
        send(got, got, sibling, ("sibling", item, 1, 0), lambda: there(item))

    def diagonal(item):
        for q in range(1, across):
            for h in pieces(item):
                got = part(block(item, 1, across - q), h)
                arrive(got, ("diagonal", item, q, h))
                send(got, got, sibling, ("sibling diagonal", item, q, h), lambda: there(item))

    def from_sibling(item):
        arrive(block(item, 0, 0, 1), ("sibling", item, 0, 0))
        arrive(block(item, 1, 0, 1), ("sibling", item, 1, 0))
        for q in range(1, across):
            arrive(block(item, 0, across - q, 1), ("sibling", item, 0, q))
            for h in pieces(item):
                arrive(part(block(item, 1, across - q, 1), h), ("sibling diagonal", item, q, h))

    if columns > 1:
        climb(1)
    spread(f_ref, here)
    own = pltpu.make_async_copy(f_ref, block(here, 0, 0), local_sems.at[0])
    load_tiles = pltpu.make_async_copy(t_ref, tiles, local_sems.at[1])
    load_weight = pltpu.make_async_copy(w_ref, weight, local_sems.at[2])
    own.start()
    load_tiles.start()
    load_weight.start()

    rounds = [[here]] + [[(-1, s), (1, s)] for s in range(1, columns)]
    for s in range(len(rounds) + 2):
        if s + 1 < columns and s > 0:
            wait_climb(s)
            climb(s + 1)
        for stage, at in ((receive, s), (relay, s - 1), (diagonal, s - 2)):
            if 0 <= at < len(rounds) and not (stage is receive and at == 0):
                for item in rounds[at]:
                    only(there(item), functools.partial(stage, item))
    for items in rounds:
        for item in items:
            only(there(item), functools.partial(from_sibling, item))
    own.wait()
    load_tiles.wait()
    load_weight.wait()

    number = tiles.shape[1]
    group = GROUP if number % GROUP == 0 else 1

    def step(i, total):
        left = jnp.concatenate([tiles[0, i * group + g] for g in range(group)], axis=1)
        right = jnp.concatenate([blocks[col_ref[0, i * group + g]] for g in range(group)], axis=0)
        return total + jnp.dot(left, right, preferred_element_type=jnp.float32)

    total = lax.fori_loop(0, number // group, step, jnp.zeros(out_ref.shape, jnp.float32), unroll=True)
    aggregated = total.astype(jnp.bfloat16)
    product = jnp.dot(aggregated, weight[...], preferred_element_type=jnp.float32)
    out_ref[...] = jnp.maximum(product, 0.0).astype(out_ref.dtype)

    if columns > 1:
        wait_climb(columns - 1)
    for rows, key, condition in sent:
        only(condition(), functools.partial(gone, rows, key))


def on_device(sections, reps, features, tiles, columns, weight):
    along, across = sections // 2, reps // 2
    side, width = features.shape
    arriving = len(arrivals(along, across))
    return pl.pallas_call(
        functools.partial(kernel, along, across),
        out_shape=jax.ShapeDtypeStruct((side, weight.shape[1]), jnp.bfloat16),
        in_specs=[pl.BlockSpec(memory_space=pltpu.SMEM)] + [pl.BlockSpec(memory_space=pltpu.HBM)] * 3,
        out_specs=pl.BlockSpec(memory_space=pltpu.VMEM),
        scratch_shapes=[
            pltpu.VMEM((sections * reps, side, width), features.dtype),
            pltpu.VMEM(tiles.shape, tiles.dtype),
            pltpu.VMEM(weight.shape, weight.dtype),
            pltpu.SemaphoreType.DMA((arriving,)),
            pltpu.SemaphoreType.DMA((arriving,)),
            pltpu.SemaphoreType.DMA((3,)),
        ],
        compiler_params=pltpu.CompilerParams(
            collective_id=0, has_side_effects=True, vmem_limit_bytes=56 * 1024 * 1024),
        cost_estimate=pl.CostEstimate(
            flops=2 * tiles.size * width, bytes_accessed=2 * (tiles.size + features.size * sections * reps),
            transcendentals=0),
    )(columns, features, tiles, weight)

def solution(mesh):
    return jax.shard_map(
        functools.partial(on_device, mesh.shape["section"], mesh.shape["rep"]),
        mesh=mesh,
        in_specs=(
            P(("section", "rep"), None),
            P(("section", "rep"), None, None, None),
            P(("section", "rep"), None),
            P(),
        ),
        out_specs=P(("section", "rep"), None),
        check_vma=False,
    )
```

```python
import functools
import jax
import jax.numpy as jnp
from jax import lax
from jax.experimental import pallas as pl
from jax.experimental.pallas import tpu as pltpu
from jax.sharding import PartitionSpec as P

GROUP = 8

def flip(index, wanted):
    return index + wanted - 2 * wanted * (index % 2)

def steps_of(columns):
    return [(0, 0)] + [(side, s) for s in range(1, columns) for side in (-1, 1)]

def arrivals(columns, across):
    keys = []
    for item in steps_of(columns):
        if item[1]:
            keys.append(("column", item))
        keys.append(("beside", item))
        keys.append(("sibling", item, 0, 0))
        keys.append(("sibling", item, 1, 0))
        for q in range(1, across):
            keys.append(("across", item, q))
            keys.extend(("diagonal", item, q, h) for h in range(3))
            keys.append(("sibling", item, 0, q))
            keys.extend(("sibling diagonal", item, q, h) for h in range(3))
    return {key: spot for spot, key in enumerate(keys)}

def kernel(columns, across, c_ref, f_ref, t_ref, w_ref, out_ref, blocks, tiles, weight, col_ref, send_sems, recv_sems, local_sems):
    rep = 2 * across
    side_rows = blocks.shape[1]
    half = side_rows // 2
    section_at = lax.axis_index("section")
    rep_at = lax.axis_index("rep")
    a, b = section_at // 2, section_at % 2
    x, c = rep_at // 2, rep_at % 2
    spots = arrivals(columns, across)
    sent, climbed = [], []

    def device(item, beside, q, other):
        at = lax.rem(x + q, across) if q else x
        return (a + item[0] * item[1]) * 2 + flip(b, beside), at * 2 + flip(c, other)

    here = (0, 0)

    def block(item, beside, q, other=0):
        s, r = device(item, beside, q, other)
        return blocks.at[s * rep + r]

    def direct(item):
        return item[1] in (0, columns - 1)

    def pieces(item):
        return (0,) if direct(item) else (1, 2)

    def part(ref, h):
        if h == 0:
            return ref
        h = h - 1
        return ref.at[pl.ds(h * half, half)]

    def there(item):
        if item[1] == 0:
            return None
        return a >= item[1] if item[0] < 0 else a + item[1] < columns

    def only(condition, work):
        if condition is None:
            work()
        else:
            pl.when(condition)(work)

    def send(src, dst, to, key, condition):
        copy = pltpu.make_async_remote_copy(
            src_ref=src, dst_ref=dst, send_sem=send_sems.at[spots[key]], recv_sem=recv_sems.at[spots[key]],
            device_id=to, device_id_type=pl.DeviceIdType.MESH)
        copy.start()
        if condition is not None:
            sent.append((src.shape[0], key, condition))

    def arrive(dst, key):
        pltpu.make_async_remote_copy(
            src_ref=dst, dst_ref=dst, send_sem=send_sems.at[0], recv_sem=recv_sems.at[spots[key]],
            device_id=device(here, 0, 0, 1), device_id_type=pl.DeviceIdType.MESH).wait_recv()

    def gone(rows, key):
        src = blocks.at[0, pl.ds(0, rows)]
        pltpu.make_async_remote_copy(
            src_ref=src, dst_ref=src, send_sem=send_sems.at[spots[key]], recv_sem=recv_sems.at[spots[key]],
            device_id=device(here, 0, 0, 1), device_id_type=pl.DeviceIdType.MESH).wait_send()

    sibling = device(here, 0, 0, 1)
    beside = device(here, 1, 0, 0)

    barrier = pltpu.get_barrier_semaphore()

    def greet(partner):
        pl.semaphore_signal(barrier, inc=1, device_id=partner, device_id_type=pl.DeviceIdType.MESH)

    partners = [device(here, 0, q, 0) for q in range(1, across)] + [beside, sibling]
    partners += [device(here, 1, q, 0) for q in range(1, across)]
    partners += [(lax.rem(a + d, columns) * 2 + b, rep_at) for d in range(1, columns)]
    for partner in partners:
        greet(partner)
    pl.semaphore_wait(barrier, len(partners))

    def climb(s):
        for side, condition in ((-1, a + s < columns), (1, a >= s)):
            to, key = device((-side, s), 0, 0, 0), ("column", (side, s))
            only(condition, functools.partial(send, f_ref, block(here, 0, 0), to, key, None))
            climbed.append((s, key, condition))

    def wait_climb(s):
        for distance, key, condition in climbed:
            if distance == s:
                only(condition, functools.partial(gone, f_ref.shape[0], key))

    def spread(src, item):
        dst = block(item, 0, 0)
        for q in range(1, across):
            send(src, dst, device(here, 0, q, 0), ("across", item, q), lambda: there(item))
        send(src, dst, beside, ("beside", item), lambda: there(item))
        if direct(item):
            for q in range(1, across):
                send(src, dst, device(here, 1, q, 0), ("diagonal", item, q, 0), lambda: there(item))
        send(src, dst, sibling, ("sibling", item, 0, 0), lambda: there(item))

    def receive(item):
        got = block(item, 0, 0)
        arrive(got, ("column", item))
        spread(got, item)

    def relay(item):
        for q in range(1, across):
            got = block(item, 0, across - q)
            arrive(got, ("across", item, q))
            if not direct(item):
                send(part(got, 1), part(got, 1), beside, ("diagonal", item, q, 1), lambda: there(item))
            send(got, got, sibling, ("sibling", item, 0, q), lambda: there(item))
        got = block(item, 1, 0)
        arrive(got, ("beside", item))
        for q in range(1, across):
            if not direct(item):
                send(part(got, 2), part(got, 2), device(here, 0, q, 0), ("diagonal", item, q, 2), lambda: there(item))
        send(got, got, sibling, ("sibling", item, 1, 0), lambda: there(item))

    def diagonal(item):
        for q in range(1, across):
            for h in pieces(item):
                got = part(block(item, 1, across - q), h)
                arrive(got, ("diagonal", item, q, h))
                send(got, got, sibling, ("sibling diagonal", item, q, h), lambda: there(item))

    def from_sibling(item):
        arrive(block(item, 0, 0, 1), ("sibling", item, 0, 0))
        arrive(block(item, 1, 0, 1), ("sibling", item, 1, 0))
        for q in range(1, across):
            arrive(block(item, 0, across - q, 1), ("sibling", item, 0, q))
            for h in pieces(item):
                arrive(part(block(item, 1, across - q, 1), h), ("sibling diagonal", item, q, h))

    if columns > 1:
        climb(1)
    spread(f_ref, here)
    own = pltpu.make_async_copy(f_ref, block(here, 0, 0), local_sems.at[0])
    load_tiles = pltpu.make_async_copy(t_ref, tiles, local_sems.at[1])
    load_weight = pltpu.make_async_copy(w_ref, weight, local_sems.at[2])
    load_columns = pltpu.make_async_copy(c_ref, col_ref, local_sems.at[3])
    own.start()
    load_columns.start()
    load_tiles.start()
    load_weight.start()

    rounds = [[here]] + [[(-1, s), (1, s)] for s in range(1, columns)]
    for s in range(len(rounds) + 2):
        if s + 1 < columns and s > 0:
            wait_climb(s)
            climb(s + 1)
        for stage, at in ((receive, s), (relay, s - 1), (diagonal, s - 2)):
            if 0 <= at < len(rounds) and not (stage is receive and at == 0):
                for item in rounds[at]:
                    only(there(item), functools.partial(stage, item))
    for items in rounds:
        for item in items:
            only(there(item), functools.partial(from_sibling, item))
    own.wait()
    load_columns.wait()
    load_tiles.wait()
    load_weight.wait()

    number = tiles.shape[1]
    group = GROUP if number % GROUP == 0 else 1

    def step(i, total):
        left = jnp.concatenate([tiles[0, i * group + g] for g in range(group)], axis=1)
        right = jnp.concatenate([blocks[col_ref[0, i * group + g]] for g in range(group)], axis=0)
        return total + jnp.dot(left, right, preferred_element_type=jnp.float32)

    total = lax.fori_loop(0, number // group, step, jnp.zeros(out_ref.shape, jnp.float32))
    aggregated = total.astype(jnp.bfloat16)
    product = jnp.dot(aggregated, weight[...], preferred_element_type=jnp.float32)
    out_ref[...] = jnp.maximum(product, 0.0).astype(out_ref.dtype)

    if columns > 1:
        wait_climb(columns - 1)
    for rows, key, condition in sent:
        only(condition(), functools.partial(gone, rows, key))


def on_device(sections, reps, features, tiles, columns, weight):
    along, across = sections // 2, reps // 2
    side, width = features.shape
    arriving = len(arrivals(along, across))
    return pl.pallas_call(
        functools.partial(kernel, along, across),
        out_shape=pltpu.VMEM((side, weight.shape[1]), jnp.bfloat16),
        in_specs=[pl.BlockSpec(memory_space=pltpu.HBM)] * 4,
        out_specs=pl.BlockSpec(memory_space=pltpu.VMEM),
        scratch_shapes=[
            pltpu.VMEM((sections * reps, side, width), features.dtype),
            pltpu.VMEM(tiles.shape, tiles.dtype),
            pltpu.VMEM(weight.shape, weight.dtype),
            pltpu.SMEM(columns.shape, columns.dtype),
            pltpu.SemaphoreType.DMA((arriving,)),
            pltpu.SemaphoreType.DMA((arriving,)),
            pltpu.SemaphoreType.DMA((4,)),
        ],
        compiler_params=pltpu.CompilerParams(
            collective_id=0, has_side_effects=True, vmem_limit_bytes=56 * 1024 * 1024),
        cost_estimate=pl.CostEstimate(
            flops=2 * tiles.size * width, bytes_accessed=2 * (tiles.size + features.size * sections * reps),
            transcendentals=0),
    )(columns, features, tiles, weight)

def solution(mesh):
    return jax.shard_map(
        functools.partial(on_device, mesh.shape["section"], mesh.shape["rep"]),
        mesh=mesh,
        in_specs=(
            P(("section", "rep"), None),
            P(("section", "rep"), None, None, None),
            P(("section", "rep"), None),
            P(),
        ),
        out_specs=P(("section", "rep"), None),
        check_vma=False,
    )
```

```python
import functools
import jax
import jax.numpy as jnp
from jax import lax
from jax.experimental import pallas as pl
from jax.experimental.pallas import tpu as pltpu
from jax.sharding import PartitionSpec as P

GROUP = 8

def flip(index, wanted):
    return index + wanted - 2 * wanted * (index % 2)

def steps_of(columns):
    return [(0, 0)] + [(side, s) for s in range(1, columns) for side in (-1, 1)]

def arrivals(columns, across):
    keys = []
    for item in steps_of(columns):
        if item[1]:
            keys.append(("column", item))
        keys.append(("beside", item))
        keys.append(("sibling", item, 0, 0))
        keys.append(("sibling", item, 1, 0))
        for q in range(1, across):
            keys.append(("across", item, q))
            keys.extend(("diagonal", item, q, h) for h in range(3))
            keys.append(("sibling", item, 0, q))
            keys.extend(("sibling diagonal", item, q, h) for h in range(3))
    return {key: spot for spot, key in enumerate(keys)}

def kernel(columns, across, c_ref, f_ref, t_ref, w_ref, out_ref, blocks, tiles, weight, col_ref, send_sems, recv_sems, local_sems):
    rep = 2 * across
    side_rows = blocks.shape[1]
    half = side_rows // 2
    section_at = lax.axis_index("section")
    rep_at = lax.axis_index("rep")
    a, b = section_at // 2, section_at % 2
    x, c = rep_at // 2, rep_at % 2
    spots = arrivals(columns, across)
    sent, climbed = [], []

    def device(item, beside, q, other):
        at = lax.rem(x + q, across) if q else x
        return (a + item[0] * item[1]) * 2 + flip(b, beside), at * 2 + flip(c, other)

    here = (0, 0)

    def block(item, beside, q, other=0):
        s, r = device(item, beside, q, other)
        return blocks.at[s * rep + r]

    def direct(item):
        return item[1] > 1 and item[1] == columns - 1

    def pieces(item):
        return (0,) if direct(item) else (1, 2)

    def part(ref, h):
        if h == 0:
            return ref
        h = h - 1
        return ref.at[pl.ds(h * half, half)]

    def there(item):
        if item[1] == 0:
            return None
        return a >= item[1] if item[0] < 0 else a + item[1] < columns

    def only(condition, work):
        if condition is None:
            work()
        else:
            pl.when(condition)(work)

    def send(src, dst, to, key, condition):
        copy = pltpu.make_async_remote_copy(
            src_ref=src, dst_ref=dst, send_sem=send_sems.at[spots[key]], recv_sem=recv_sems.at[spots[key]],
            device_id=to, device_id_type=pl.DeviceIdType.MESH)
        copy.start()
        if condition is not None:
            sent.append((src.shape[0], key, condition))

    def arrive(dst, key):
        pltpu.make_async_remote_copy(
            src_ref=dst, dst_ref=dst, send_sem=send_sems.at[0], recv_sem=recv_sems.at[spots[key]],
            device_id=device(here, 0, 0, 1), device_id_type=pl.DeviceIdType.MESH).wait_recv()

    def gone(rows, key):
        src = blocks.at[0, pl.ds(0, rows)]
        pltpu.make_async_remote_copy(
            src_ref=src, dst_ref=src, send_sem=send_sems.at[spots[key]], recv_sem=recv_sems.at[spots[key]],
            device_id=device(here, 0, 0, 1), device_id_type=pl.DeviceIdType.MESH).wait_send()

    sibling = device(here, 0, 0, 1)
    beside = device(here, 1, 0, 0)

    barrier = pltpu.get_barrier_semaphore()

    def greet(partner):
        pl.semaphore_signal(barrier, inc=1, device_id=partner, device_id_type=pl.DeviceIdType.MESH)

    partners = [device(here, 0, q, 0) for q in range(1, across)] + [beside, sibling]
    partners += [device(here, 1, q, 0) for q in range(1, across)]
    partners += [(lax.rem(a + d, columns) * 2 + b, rep_at) for d in range(1, columns)]
    for partner in partners:
        greet(partner)
    pl.semaphore_wait(barrier, len(partners))

    def climb(s):
        for side, condition in ((-1, a + s < columns), (1, a >= s)):
            to, key = device((-side, s), 0, 0, 0), ("column", (side, s))
            only(condition, functools.partial(send, f_ref, block(here, 0, 0), to, key, None))
            climbed.append((s, key, condition))

    def wait_climb(s):
        for distance, key, condition in climbed:
            if distance == s:
                only(condition, functools.partial(gone, f_ref.shape[0], key))

    def pass_on(src, item):
        on = a + 1 < columns if item[0] < 0 else a >= 1
        to, key = device((-item[0], 1), 0, 0, 0), ("column", (item[0], 2))
        only(on, lambda: send(src, src, to, key, None))

    def spread(src, item):
        dst = block(item, 0, 0)
        for q in range(1, across):
            send(src, dst, device(here, 0, q, 0), ("across", item, q), lambda: there(item))
        send(src, dst, beside, ("beside", item), lambda: there(item))
        if direct(item):
            for q in range(1, across):
                send(src, dst, device(here, 1, q, 0), ("diagonal", item, q, 0), lambda: there(item))
        send(src, dst, sibling, ("sibling", item, 0, 0), lambda: there(item))

    def receive(item):
        got = block(item, 0, 0)
        arrive(got, ("column", item))
        if item[1] == 1 and columns > 2:
            pass_on(got, item)
        spread(got, item)

    def relay(item):
        for q in range(1, across):
            got = block(item, 0, across - q)
            arrive(got, ("across", item, q))
            if not direct(item):
                send(part(got, 1), part(got, 1), beside, ("diagonal", item, q, 1), lambda: there(item))
            send(got, got, sibling, ("sibling", item, 0, q), lambda: there(item))
        got = block(item, 1, 0)
        arrive(got, ("beside", item))
        for q in range(1, across):
            if not direct(item):
                send(part(got, 2), part(got, 2), device(here, 0, q, 0), ("diagonal", item, q, 2), lambda: there(item))
        send(got, got, sibling, ("sibling", item, 1, 0), lambda: there(item))

    def diagonal(item):
        for q in range(1, across):
            for h in pieces(item):
                got = part(block(item, 1, across - q), h)
                arrive(got, ("diagonal", item, q, h))
                send(got, got, sibling, ("sibling diagonal", item, q, h), lambda: there(item))

    def from_sibling(item):
        arrive(block(item, 0, 0, 1), ("sibling", item, 0, 0))
        arrive(block(item, 1, 0, 1), ("sibling", item, 1, 0))
        for q in range(1, across):
            arrive(block(item, 0, across - q, 1), ("sibling", item, 0, q))
            for h in pieces(item):
                arrive(part(block(item, 1, across - q, 1), h), ("sibling diagonal", item, q, h))

    if columns > 1:
        climb(1)
    spread(f_ref, here)
    own = pltpu.make_async_copy(f_ref, block(here, 0, 0), local_sems.at[0])
    load_tiles = pltpu.make_async_copy(t_ref, tiles, local_sems.at[1])
    load_weight = pltpu.make_async_copy(w_ref, weight, local_sems.at[2])
    load_columns = pltpu.make_async_copy(c_ref, col_ref, local_sems.at[3])
    own.start()
    load_columns.start()
    load_tiles.start()
    load_weight.start()

    for s in range(3, columns):
        wait_climb(1 if s == 3 else s - 1)
        climb(s)

    rounds = [[here]] + [[(-1, s), (1, s)] for s in range(1, columns)]
    for s in range(len(rounds) + 2):
        for stage, at in ((receive, s), (relay, s - 1), (diagonal, s - 2)):
            if 0 <= at < len(rounds) and not (stage is receive and at == 0):
                for item in rounds[at]:
                    only(there(item), functools.partial(stage, item))
    for items in rounds:
        for item in items:
            only(there(item), functools.partial(from_sibling, item))
    own.wait()
    load_columns.wait()
    load_tiles.wait()
    load_weight.wait()

    number = tiles.shape[1]
    group = GROUP if number % GROUP == 0 else 1

    def step(i, total):
        left = jnp.concatenate([tiles[0, i * group + g] for g in range(group)], axis=1)
        right = jnp.concatenate([blocks[col_ref[0, i * group + g]] for g in range(group)], axis=0)
        return total + jnp.dot(left, right, preferred_element_type=jnp.float32)

    total = lax.fori_loop(0, number // group, step, jnp.zeros(out_ref.shape, jnp.float32))
    aggregated = total.astype(jnp.bfloat16)
    product = jnp.dot(aggregated, weight[...], preferred_element_type=jnp.float32)
    out_ref[...] = jnp.maximum(product, 0.0).astype(out_ref.dtype)

    if columns > 1:
        wait_climb(columns - 1 if columns > 3 else 1)
    if columns > 2:
        for item, condition in (((-1, 2), (a >= 1) & (a + 1 < columns)), ((1, 2), (a >= 1) & (a + 1 < columns))):
            only(condition, functools.partial(gone, f_ref.shape[0], ("column", item)))
    for rows, key, condition in sent:
        only(condition(), functools.partial(gone, rows, key))


def on_device(sections, reps, features, tiles, columns, weight):
    along, across = sections // 2, reps // 2
    side, width = features.shape
    arriving = len(arrivals(along, across))
    return pl.pallas_call(
        functools.partial(kernel, along, across),
        out_shape=pltpu.VMEM((side, weight.shape[1]), jnp.bfloat16),
        in_specs=[pl.BlockSpec(memory_space=pltpu.HBM)] * 4,
        out_specs=pl.BlockSpec(memory_space=pltpu.VMEM),
        scratch_shapes=[
            pltpu.VMEM((sections * reps, side, width), features.dtype),
            pltpu.VMEM(tiles.shape, tiles.dtype),
            pltpu.VMEM(weight.shape, weight.dtype),
            pltpu.SMEM(columns.shape, columns.dtype),
            pltpu.SemaphoreType.DMA((arriving,)),
            pltpu.SemaphoreType.DMA((arriving,)),
            pltpu.SemaphoreType.DMA((4,)),
        ],
        compiler_params=pltpu.CompilerParams(
            collective_id=0, has_side_effects=True, vmem_limit_bytes=56 * 1024 * 1024),
        cost_estimate=pl.CostEstimate(
            flops=2 * tiles.size * width, bytes_accessed=2 * (tiles.size + features.size * sections * reps),
            transcendentals=0),
    )(columns, features, tiles, weight)

def solution(mesh):
    return jax.shard_map(
        functools.partial(on_device, mesh.shape["section"], mesh.shape["rep"]),
        mesh=mesh,
        in_specs=(
            P(("section", "rep"), None),
            P(("section", "rep"), None, None, None),
            P(("section", "rep"), None),
            P(),
        ),
        out_specs=P(("section", "rep"), None),
        check_vma=False,
    )
```

```python
import functools
import jax
import jax.numpy as jnp
from jax import lax
from jax.experimental import pallas as pl
from jax.experimental.pallas import tpu as pltpu
from jax.sharding import PartitionSpec as P

GROUP = 8

def flip(index, wanted):
    return index + wanted - 2 * wanted * (index % 2)

def steps_of(columns):
    return [(0, 0)] + [(side, s) for s in range(1, columns) for side in (-1, 1)]

def arrivals(columns, across):
    keys = []
    for item in steps_of(columns):
        if item[1]:
            keys.append(("column", item))
        keys.append(("beside", item))
        keys.append(("sibling", item, 0, 0))
        keys.append(("sibling", item, 1, 0))
        for q in range(1, across):
            keys.append(("across", item, q))
            keys.extend(("diagonal", item, q, h) for h in range(3))
            keys.append(("sibling", item, 0, q))
            keys.extend(("sibling diagonal", item, q, h) for h in range(3))
    return {key: spot for spot, key in enumerate(keys)}

def kernel(columns, across, c_ref, f_ref, t_ref, w_ref, out_ref, blocks, tiles, weight, col_ref, send_sems, recv_sems, local_sems):
    rep = 2 * across
    side_rows = blocks.shape[1]
    half = side_rows // 2
    section_at = lax.axis_index("section")
    rep_at = lax.axis_index("rep")
    a, b = section_at // 2, section_at % 2
    x, c = rep_at // 2, rep_at % 2
    spots = arrivals(columns, across)
    sent, climbed = [], []

    def device(item, beside, q, other):
        at = lax.rem(x + q, across) if q else x
        return (a + item[0] * item[1]) * 2 + flip(b, beside), at * 2 + flip(c, other)

    here = (0, 0)

    def block(item, beside, q, other=0):
        s, r = device(item, beside, q, other)
        return blocks.at[s * rep + r]

    def direct(item):
        return item[1] > 1 and item[1] == columns - 1

    def pieces(item):
        return (0,) if direct(item) else (1, 2)

    def part(ref, h):
        if h == 0:
            return ref
        h = h - 1
        return ref.at[pl.ds(h * half, half)]

    def there(item):
        if item[1] == 0:
            return None
        return a >= item[1] if item[0] < 0 else a + item[1] < columns

    def only(condition, work):
        if condition is None:
            work()
        else:
            pl.when(condition)(work)

    def send(src, dst, to, key, condition):
        copy = pltpu.make_async_remote_copy(
            src_ref=src, dst_ref=dst, send_sem=send_sems.at[spots[key]], recv_sem=recv_sems.at[spots[key]],
            device_id=to, device_id_type=pl.DeviceIdType.MESH)
        copy.start()
        if condition is not None:
            sent.append((src.shape[0], key, condition))

    def arrive(dst, key):
        pltpu.make_async_remote_copy(
            src_ref=dst, dst_ref=dst, send_sem=send_sems.at[0], recv_sem=recv_sems.at[spots[key]],
            device_id=device(here, 0, 0, 1), device_id_type=pl.DeviceIdType.MESH).wait_recv()

    def gone(rows, key):
        src = blocks.at[0, pl.ds(0, rows)]
        pltpu.make_async_remote_copy(
            src_ref=src, dst_ref=src, send_sem=send_sems.at[spots[key]], recv_sem=recv_sems.at[spots[key]],
            device_id=device(here, 0, 0, 1), device_id_type=pl.DeviceIdType.MESH).wait_send()

    sibling = device(here, 0, 0, 1)
    beside = device(here, 1, 0, 0)

    barrier = pltpu.get_barrier_semaphore()

    def greet(partner):
        pl.semaphore_signal(barrier, inc=1, device_id=partner, device_id_type=pl.DeviceIdType.MESH)

    partners = [device(here, 0, q, 0) for q in range(1, across)] + [beside, sibling]
    partners += [device(here, 1, q, 0) for q in range(1, across)]
    partners += [(lax.rem(a + d, columns) * 2 + b, rep_at) for d in range(1, columns)]
    for partner in partners:
        greet(partner)
    pl.semaphore_wait(barrier, len(partners))

    def climb(s):
        for side, condition in ((-1, a + s < columns), (1, a >= s)):
            to, key = device((-side, s), 0, 0, 0), ("column", (side, s))
            only(condition, functools.partial(send, f_ref, block(here, 0, 0), to, key, None))
            climbed.append((s, key, condition))

    def wait_climb(s):
        for distance, key, condition in climbed:
            if distance == s:
                only(condition, functools.partial(gone, f_ref.shape[0], key))

    def pass_on(src, item):
        on = a + 1 < columns if item[0] < 0 else a >= 1
        to, key = device((-item[0], 1), 0, 0, 0), ("column", (item[0], 2))
        only(on, lambda: send(src, src, to, key, None))

    def spread(src, item):
        dst = block(item, 0, 0)
        for q in range(1, across):
            send(src, dst, device(here, 0, q, 0), ("across", item, q), lambda: there(item))
        send(src, dst, beside, ("beside", item), lambda: there(item))
        if direct(item):
            for q in range(1, across):
                send(src, dst, device(here, 1, q, 0), ("diagonal", item, q, 0), lambda: there(item))
        send(src, dst, sibling, ("sibling", item, 0, 0), lambda: there(item))

    def receive(item):
        got = block(item, 0, 0)
        arrive(got, ("column", item))
        if item[1] == 1 and columns > 2:
            pass_on(got, item)
        spread(got, item)

    def relay(item):
        for q in range(1, across):
            got = block(item, 0, across - q)
            arrive(got, ("across", item, q))
            if not direct(item):
                send(part(got, 1), part(got, 1), beside, ("diagonal", item, q, 1), lambda: there(item))
            send(got, got, sibling, ("sibling", item, 0, q), lambda: there(item))
        got = block(item, 1, 0)
        arrive(got, ("beside", item))
        for q in range(1, across):
            if not direct(item):
                send(part(got, 2), part(got, 2), device(here, 0, q, 0), ("diagonal", item, q, 2), lambda: there(item))
        send(got, got, sibling, ("sibling", item, 1, 0), lambda: there(item))

    def diagonal(item):
        for q in range(1, across):
            for h in pieces(item):
                got = part(block(item, 1, across - q), h)
                arrive(got, ("diagonal", item, q, h))
                send(got, got, sibling, ("sibling diagonal", item, q, h), lambda: there(item))

    def from_sibling(item):
        arrive(block(item, 0, 0, 1), ("sibling", item, 0, 0))
        arrive(block(item, 1, 0, 1), ("sibling", item, 1, 0))
        for q in range(1, across):
            arrive(block(item, 0, across - q, 1), ("sibling", item, 0, q))
            for h in pieces(item):
                arrive(part(block(item, 1, across - q, 1), h), ("sibling diagonal", item, q, h))

    if columns > 1:
        climb(1)
    spread(f_ref, here)
    own = pltpu.make_async_copy(f_ref, block(here, 0, 0), local_sems.at[0])
    load_tiles = pltpu.make_async_copy(t_ref, tiles, local_sems.at[1])
    load_weight = pltpu.make_async_copy(w_ref, weight, local_sems.at[2])
    load_columns = pltpu.make_async_copy(c_ref, col_ref, local_sems.at[3])
    own.start()
    load_columns.start()
    load_tiles.start()
    load_weight.start()

    for s in range(3, columns):
        wait_climb(1 if s == 3 else s - 1)
        climb(s)

    rounds = [[here]] + [[(-1, s), (1, s)] for s in range(1, columns)]
    for s in range(len(rounds) + 2):
        for stage, at in ((receive, s), (relay, s - 1), (diagonal, s - 2)):
            if 0 <= at < len(rounds) and not (stage is receive and at == 0):
                for item in rounds[at]:
                    only(there(item), functools.partial(stage, item))
    for items in rounds:
        for item in items:
            only(there(item), functools.partial(from_sibling, item))
    own.wait()
    load_columns.wait()
    load_tiles.wait()
    load_weight.wait()

    number = tiles.shape[1]
    group = GROUP if number % GROUP == 0 else 1

    def step(i, total):
        left = jnp.concatenate([tiles[0, i * group + g] for g in range(group)], axis=1)
        right = jnp.concatenate([blocks[col_ref[0, i * group + g]] for g in range(group)], axis=0)
        return total + jnp.dot(left, right, preferred_element_type=jnp.float32)

    total = lax.fori_loop(0, number // group, step, jnp.zeros(out_ref.shape, jnp.float32), unroll=True)
    aggregated = total.astype(jnp.bfloat16)
    product = jnp.dot(aggregated, weight[...], preferred_element_type=jnp.float32)
    out_ref[...] = jnp.maximum(product, 0.0).astype(out_ref.dtype)

    if columns > 1:
        wait_climb(columns - 1 if columns > 3 else 1)
    if columns > 2:
        for item, condition in (((-1, 2), (a >= 1) & (a + 1 < columns)), ((1, 2), (a >= 1) & (a + 1 < columns))):
            only(condition, functools.partial(gone, f_ref.shape[0], ("column", item)))
    for rows, key, condition in sent:
        only(condition(), functools.partial(gone, rows, key))


def on_device(sections, reps, features, tiles, columns, weight):
    along, across = sections // 2, reps // 2
    side, width = features.shape
    arriving = len(arrivals(along, across))
    return pl.pallas_call(
        functools.partial(kernel, along, across),
        out_shape=pltpu.VMEM((side, weight.shape[1]), jnp.bfloat16),
        in_specs=[pl.BlockSpec(memory_space=pltpu.HBM)] * 4,
        out_specs=pl.BlockSpec(memory_space=pltpu.VMEM),
        scratch_shapes=[
            pltpu.VMEM((sections * reps, side, width), features.dtype),
            pltpu.VMEM(tiles.shape, tiles.dtype),
            pltpu.VMEM(weight.shape, weight.dtype),
            pltpu.SMEM(columns.shape, columns.dtype),
            pltpu.SemaphoreType.DMA((arriving,)),
            pltpu.SemaphoreType.DMA((arriving,)),
            pltpu.SemaphoreType.DMA((4,)),
        ],
        compiler_params=pltpu.CompilerParams(
            collective_id=0, has_side_effects=True, vmem_limit_bytes=56 * 1024 * 1024),
        cost_estimate=pl.CostEstimate(
            flops=2 * tiles.size * width, bytes_accessed=2 * (tiles.size + features.size * sections * reps),
            transcendentals=0),
    )(columns, features, tiles, weight)

def solution(mesh):
    return jax.shard_map(
        functools.partial(on_device, mesh.shape["section"], mesh.shape["rep"]),
        mesh=mesh,
        in_specs=(
            P(("section", "rep"), None),
            P(("section", "rep"), None, None, None),
            P(("section", "rep"), None),
            P(),
        ),
        out_specs=P(("section", "rep"), None),
        check_vma=False,
    )
```

```python
import functools
import jax
import jax.numpy as jnp
from jax import lax
from jax.experimental import pallas as pl
from jax.experimental.pallas import tpu as pltpu
from jax.sharding import PartitionSpec as P

GROUP = 8

def flip(index, wanted):
    return index + wanted - 2 * wanted * (index % 2)

def steps_of(columns):
    return [(0, 0)] + [(side, s) for s in range(1, columns) for side in (-1, 1)]

def arrivals(columns, across):
    keys = []
    for item in steps_of(columns):
        if item[1]:
            keys.append(("column", item))
        keys.append(("beside", item))
        for q in range(1, across):
            keys.append(("across", item, q))
            keys.extend(("diagonal", item, q, h) for h in range(3))
    return {key: spot for spot, key in enumerate(keys)}


def kernel(columns, across, c_ref, f_ref, t_ref, w_ref, out_ref, blocks, tiles, weight, col_ref, send_sems, recv_sems, all_sent, all_came, local_sems):
    rep = 2 * across
    side_rows = blocks.shape[1]
    half = side_rows // 2
    section_at = lax.axis_index("section")
    rep_at = lax.axis_index("rep")
    a, b = section_at // 2, section_at % 2
    x, c = rep_at // 2, rep_at % 2
    spots = arrivals(columns, across)
    climbed = []

    def device(item, beside, q, other):
        at = lax.rem(x + q, across) if q else x
        return (a + item[0] * item[1]) * 2 + flip(b, beside), at * 2 + flip(c, other)

    here = (0, 0)

    def block(item, beside, q, other=0):
        s, r = device(item, beside, q, other)
        return blocks.at[s * rep + r]

    def direct(item):
        return item[1] > 1 and item[1] == columns - 1

    def pieces(item):
        return (0,) if direct(item) else (1, 2)

    def part(ref, h):
        if h == 0:
            return ref
        h = h - 1
        return ref.at[pl.ds(h * half, half)]

    def there(item):
        if item[1] == 0:
            return None
        return a >= item[1] if item[0] < 0 else a + item[1] < columns

    def only(condition, work):
        if condition is None:
            work()
        else:
            pl.when(condition)(work)

    def send(src, dst, to, key):
        copy = pltpu.make_async_remote_copy(
            src_ref=src, dst_ref=dst, send_sem=send_sems.at[spots[key]] if key[0] == "column" else all_sent,
            recv_sem=all_came if key[0] == "sibling" else recv_sems.at[spots[key]],
            device_id=to, device_id_type=pl.DeviceIdType.MESH)
        copy.start()

    def arrive(dst, key):
        pltpu.make_async_remote_copy(
            src_ref=dst, dst_ref=dst, send_sem=send_sems.at[0], recv_sem=recv_sems.at[spots[key]],
            device_id=device(here, 0, 0, 1), device_id_type=pl.DeviceIdType.MESH).wait_recv()

    def gone(rows, key):
        src = blocks.at[0, pl.ds(0, rows)]
        pltpu.make_async_remote_copy(
            src_ref=src, dst_ref=src, send_sem=send_sems.at[spots[key]], recv_sem=recv_sems.at[spots[key]],
            device_id=device(here, 0, 0, 1), device_id_type=pl.DeviceIdType.MESH).wait_send()

    sibling = device(here, 0, 0, 1)
    beside = device(here, 1, 0, 0)

    barrier = pltpu.get_barrier_semaphore()

    def greet(partner):
        pl.semaphore_signal(barrier, inc=1, device_id=partner, device_id_type=pl.DeviceIdType.MESH)

    partners = [device(here, 0, q, 0) for q in range(1, across)] + [beside, sibling]
    partners += [device(here, 1, q, 0) for q in range(1, across)]
    partners += [(lax.rem(a + d, columns) * 2 + b, rep_at) for d in range(1, columns)]
    for partner in partners:
        greet(partner)
    pl.semaphore_wait(barrier, len(partners))

    def climb(s):
        for side, condition in ((-1, a + s < columns), (1, a >= s)):
            to, key = device((-side, s), 0, 0, 0), ("column", (side, s))
            only(condition, functools.partial(send, f_ref, block(here, 0, 0), to, key))
            climbed.append((s, key, condition))

    def wait_climb(s):
        for distance, key, condition in climbed:
            if distance == s:
                only(condition, functools.partial(gone, f_ref.shape[0], key))

    def pass_on(src, item):
        on = a + 1 < columns if item[0] < 0 else a >= 1
        to, key = device((-item[0], 1), 0, 0, 0), ("column", (item[0], 2))
        only(on, lambda: send(src, src, to, key))

    def spread(src, item):
        dst = block(item, 0, 0)
        for q in range(1, across):
            send(src, dst, device(here, 0, q, 0), ("across", item, q))
        send(src, dst, beside, ("beside", item))
        if direct(item):
            for q in range(1, across):
                send(src, dst, device(here, 1, q, 0), ("diagonal", item, q, 0))
        send(src, dst, sibling, ("sibling",))

    def receive(item):
        got = block(item, 0, 0)
        arrive(got, ("column", item))
        if item[1] == 1 and columns > 2:
            pass_on(got, item)
        spread(got, item)

    def relay(item):
        for q in range(1, across):
            got = block(item, 0, across - q)
            arrive(got, ("across", item, q))
            if not direct(item):
                send(part(got, 1), part(got, 1), beside, ("diagonal", item, q, 1))
            send(got, got, sibling, ("sibling",))
        got = block(item, 1, 0)
        arrive(got, ("beside", item))
        for q in range(1, across):
            if not direct(item):
                send(part(got, 2), part(got, 2), device(here, 0, q, 0), ("diagonal", item, q, 2))
        send(got, got, sibling, ("sibling",))

    def diagonal(item):
        for q in range(1, across):
            for h in pieces(item):
                got = part(block(item, 1, across - q), h)
                arrive(got, ("diagonal", item, q, h))
                send(got, got, sibling, ("sibling",))

    if columns > 1:
        climb(1)
    spread(f_ref, here)
    own = pltpu.make_async_copy(f_ref, block(here, 0, 0), local_sems.at[0])
    load_tiles = pltpu.make_async_copy(t_ref, tiles, local_sems.at[1])
    load_weight = pltpu.make_async_copy(w_ref, weight, local_sems.at[2])
    load_columns = pltpu.make_async_copy(c_ref, col_ref, local_sems.at[3])
    own.start()
    load_columns.start()
    load_tiles.start()
    load_weight.start()

    for s in range(3, columns):
        wait_climb(1 if s == 3 else s - 1)
        climb(s)

    rounds = [[here]] + [[(-1, s), (1, s)] for s in range(1, columns)]
    for s in range(len(rounds) + 2):
        for stage, at in ((receive, s), (relay, s - 1), (diagonal, s - 2)):
            if 0 <= at < len(rounds) and not (stage is receive and at == 0):
                for item in rounds[at]:
                    only(there(item), functools.partial(stage, item))
    whole = blocks.at[pl.ds(0, columns * 2 * across)]
    pltpu.make_async_remote_copy(
        src_ref=whole, dst_ref=whole, send_sem=all_sent, recv_sem=all_came,
        device_id=sibling, device_id_type=pl.DeviceIdType.MESH).wait_recv()
    own.wait()
    load_columns.wait()
    load_tiles.wait()
    load_weight.wait()

    number = tiles.shape[1]
    group = GROUP if number % GROUP == 0 else 1

    def step(i, total):
        left = jnp.concatenate([tiles[0, i * group + g] for g in range(group)], axis=1)
        right = jnp.concatenate([blocks[col_ref[0, i * group + g]] for g in range(group)], axis=0)
        return total + jnp.dot(left, right, preferred_element_type=jnp.float32)

    total = lax.fori_loop(0, number // group, step, jnp.zeros(out_ref.shape, jnp.float32), unroll=True)
    aggregated = total.astype(jnp.bfloat16)
    product = jnp.dot(aggregated, weight[...], preferred_element_type=jnp.float32)
    out_ref[...] = jnp.maximum(product, 0.0).astype(out_ref.dtype)

    if columns > 1:
        wait_climb(columns - 1 if columns > 3 else 1)
    if columns > 2:
        for item, condition in (((-1, 2), (a >= 1) & (a + 1 < columns)), ((1, 2), (a >= 1) & (a + 1 < columns))):
            only(condition, functools.partial(gone, f_ref.shape[0], ("column", item)))
    whole = blocks.at[pl.ds(0, columns * (4 * across - 1))]
    pltpu.make_async_remote_copy(
        src_ref=whole, dst_ref=whole, send_sem=all_sent, recv_sem=all_came,
        device_id=sibling, device_id_type=pl.DeviceIdType.MESH).wait_send()


def on_device(sections, reps, features, tiles, columns, weight):
    along, across = sections // 2, reps // 2
    side, width = features.shape
    arriving = len(arrivals(along, across))
    return pl.pallas_call(
        functools.partial(kernel, along, across),
        out_shape=pltpu.VMEM((side, weight.shape[1]), jnp.bfloat16),
        in_specs=[pl.BlockSpec(memory_space=pltpu.HBM)] * 4,
        out_specs=pl.BlockSpec(memory_space=pltpu.VMEM),
        scratch_shapes=[
            pltpu.VMEM((sections * reps, side, width), features.dtype),
            pltpu.VMEM(tiles.shape, tiles.dtype),
            pltpu.VMEM(weight.shape, weight.dtype),
            pltpu.SMEM(columns.shape, columns.dtype),
            pltpu.SemaphoreType.DMA((arriving,)),
            pltpu.SemaphoreType.DMA((arriving,)),
            pltpu.SemaphoreType.DMA,
            pltpu.SemaphoreType.DMA,
            pltpu.SemaphoreType.DMA((4,)),
        ],
        compiler_params=pltpu.CompilerParams(
            collective_id=0, has_side_effects=True, vmem_limit_bytes=56 * 1024 * 1024),
        cost_estimate=pl.CostEstimate(
            flops=2 * tiles.size * width, bytes_accessed=2 * (tiles.size + features.size * sections * reps),
            transcendentals=0),
    )(columns, features, tiles, weight)

def solution(mesh):
    return jax.shard_map(
        functools.partial(on_device, mesh.shape["section"], mesh.shape["rep"]),
        mesh=mesh,
        in_specs=(
            P(("section", "rep"), None),
            P(("section", "rep"), None, None, None),
            P(("section", "rep"), None),
            P(),
        ),
        out_specs=P(("section", "rep"), None),
        check_vma=False,
    )
```

```python
import functools
import jax
import jax.numpy as jnp
from jax import lax
from jax.experimental import pallas as pl
from jax.experimental.pallas import tpu as pltpu
from jax.sharding import PartitionSpec as P

GROUP = 2

def flip(index, wanted):
    return index + wanted - 2 * wanted * (index % 2)

def steps_of(columns):
    return [(0, 0)] + [(side, s) for s in range(1, columns) for side in (-1, 1)]

def arrivals(columns, across):
    keys = []
    for item in steps_of(columns):
        if item[1]:
            keys.append(("column", item))
        keys.append(("beside", item))
        for q in range(1, across):
            keys.append(("across", item, q))
            keys.extend(("diagonal", item, q, h) for h in range(3))
    return {key: spot for spot, key in enumerate(keys)}


def kernel(columns, across, c_ref, f_ref, t_ref, w_ref, out_ref, blocks, tiles, weight, col_ref, send_sems, recv_sems, all_sent, all_came, local_sems):
    rep = 2 * across
    side_rows = blocks.shape[1]
    half = side_rows // 2
    section_at = lax.axis_index("section")
    rep_at = lax.axis_index("rep")
    a, b = section_at // 2, section_at % 2
    x, c = rep_at // 2, rep_at % 2
    spots = arrivals(columns, across)
    climbed = []

    def device(item, beside, q, other):
        at = lax.rem(x + q, across) if q else x
        return (a + item[0] * item[1]) * 2 + flip(b, beside), at * 2 + flip(c, other)

    here = (0, 0)

    def block(item, beside, q, other=0):
        s, r = device(item, beside, q, other)
        return blocks.at[s * rep + r]

    def direct(item):
        return item[1] > 1 and item[1] == columns - 1

    def pieces(item):
        return (0,) if direct(item) else (1, 2)

    def part(ref, h):
        if h == 0:
            return ref
        h = h - 1
        return ref.at[pl.ds(h * half, half)]

    def there(item):
        if item[1] == 0:
            return None
        return a >= item[1] if item[0] < 0 else a + item[1] < columns

    def only(condition, work):
        if condition is None:
            work()
        else:
            pl.when(condition)(work)

    def send(src, dst, to, key):
        copy = pltpu.make_async_remote_copy(
            src_ref=src, dst_ref=dst, send_sem=send_sems.at[spots[key]] if key[0] == "column" else all_sent,
            recv_sem=all_came if key[0] == "sibling" else recv_sems.at[spots[key]],
            device_id=to, device_id_type=pl.DeviceIdType.MESH)
        copy.start()

    def arrive(dst, key):
        pltpu.make_async_remote_copy(
            src_ref=dst, dst_ref=dst, send_sem=send_sems.at[0], recv_sem=recv_sems.at[spots[key]],
            device_id=device(here, 0, 0, 1), device_id_type=pl.DeviceIdType.MESH).wait_recv()

    def gone(rows, key):
        src = blocks.at[0, pl.ds(0, rows)]
        pltpu.make_async_remote_copy(
            src_ref=src, dst_ref=src, send_sem=send_sems.at[spots[key]], recv_sem=recv_sems.at[spots[key]],
            device_id=device(here, 0, 0, 1), device_id_type=pl.DeviceIdType.MESH).wait_send()

    sibling = device(here, 0, 0, 1)
    beside = device(here, 1, 0, 0)

    barrier = pltpu.get_barrier_semaphore()

    def greet(partner):
        pl.semaphore_signal(barrier, inc=1, device_id=partner, device_id_type=pl.DeviceIdType.MESH)

    partners = [device(here, 0, q, 0) for q in range(1, across)] + [beside, sibling]
    partners += [device(here, 1, q, 0) for q in range(1, across)]
    partners += [(lax.rem(a + d, columns) * 2 + b, rep_at) for d in range(1, columns)]
    for partner in partners:
        greet(partner)
    pl.semaphore_wait(barrier, len(partners))

    def climb(s):
        for side, condition in ((-1, a + s < columns), (1, a >= s)):
            to, key = device((-side, s), 0, 0, 0), ("column", (side, s))
            only(condition, functools.partial(send, f_ref, block(here, 0, 0), to, key))
            climbed.append((s, key, condition))

    def wait_climb(s):
        for distance, key, condition in climbed:
            if distance == s:
                only(condition, functools.partial(gone, f_ref.shape[0], key))

    def pass_on(src, item):
        on = a + 1 < columns if item[0] < 0 else a >= 1
        to, key = device((-item[0], 1), 0, 0, 0), ("column", (item[0], 2))
        only(on, lambda: send(src, src, to, key))

    def spread(src, item):
        dst = block(item, 0, 0)
        for q in range(1, across):
            send(src, dst, device(here, 0, q, 0), ("across", item, q))
        send(src, dst, beside, ("beside", item))
        if direct(item):
            for q in range(1, across):
                send(src, dst, device(here, 1, q, 0), ("diagonal", item, q, 0))
        send(src, dst, sibling, ("sibling",))

    def receive(item):
        got = block(item, 0, 0)
        arrive(got, ("column", item))
        if item[1] == 1 and columns > 2:
            pass_on(got, item)
        spread(got, item)

    def relay(item):
        for q in range(1, across):
            got = block(item, 0, across - q)
            arrive(got, ("across", item, q))
            if not direct(item):
                send(part(got, 1), part(got, 1), beside, ("diagonal", item, q, 1))
            send(got, got, sibling, ("sibling",))
        got = block(item, 1, 0)
        arrive(got, ("beside", item))
        for q in range(1, across):
            if not direct(item):
                send(part(got, 2), part(got, 2), device(here, 0, q, 0), ("diagonal", item, q, 2))
        send(got, got, sibling, ("sibling",))

    def diagonal(item):
        for q in range(1, across):
            for h in pieces(item):
                got = part(block(item, 1, across - q), h)
                arrive(got, ("diagonal", item, q, h))
                send(got, got, sibling, ("sibling",))

    if columns > 1:
        climb(1)
    spread(f_ref, here)
    own = pltpu.make_async_copy(f_ref, block(here, 0, 0), local_sems.at[0])
    load_tiles = pltpu.make_async_copy(t_ref, tiles, local_sems.at[1])
    load_weight = pltpu.make_async_copy(w_ref, weight, local_sems.at[2])
    load_columns = pltpu.make_async_copy(c_ref, col_ref, local_sems.at[3])
    own.start()
    load_columns.start()
    load_tiles.start()
    load_weight.start()

    for s in range(3, columns):
        wait_climb(1 if s == 3 else s - 1)
        climb(s)

    rounds = [[here]] + [[(-1, s), (1, s)] for s in range(1, columns)]
    for s in range(len(rounds) + 2):
        for stage, at in ((receive, s), (relay, s - 1), (diagonal, s - 2)):
            if 0 <= at < len(rounds) and not (stage is receive and at == 0):
                for item in rounds[at]:
                    only(there(item), functools.partial(stage, item))
    whole = blocks.at[pl.ds(0, columns * 2 * across)]
    pltpu.make_async_remote_copy(
        src_ref=whole, dst_ref=whole, send_sem=all_sent, recv_sem=all_came,
        device_id=sibling, device_id_type=pl.DeviceIdType.MESH).wait_recv()
    own.wait()
    load_columns.wait()
    load_tiles.wait()
    load_weight.wait()

    number = tiles.shape[1]
    group = GROUP if number % GROUP == 0 else 1

    def step(i, total):
        left = jnp.concatenate([tiles[0, i * group + g] for g in range(group)], axis=1)
        right = jnp.concatenate([blocks[col_ref[0, i * group + g]] for g in range(group)], axis=0)
        return total + jnp.dot(left, right, preferred_element_type=jnp.float32)

    total = lax.fori_loop(0, number // group, step, jnp.zeros(out_ref.shape, jnp.float32), unroll=True)
    aggregated = total.astype(jnp.bfloat16)
    product = jnp.dot(aggregated, weight[...], preferred_element_type=jnp.float32)
    out_ref[...] = jnp.maximum(product, 0.0).astype(out_ref.dtype)

    if columns > 1:
        wait_climb(columns - 1 if columns > 3 else 1)
    if columns > 2:
        for item, condition in (((-1, 2), (a >= 1) & (a + 1 < columns)), ((1, 2), (a >= 1) & (a + 1 < columns))):
            only(condition, functools.partial(gone, f_ref.shape[0], ("column", item)))
    whole = blocks.at[pl.ds(0, columns * (4 * across - 1))]
    pltpu.make_async_remote_copy(
        src_ref=whole, dst_ref=whole, send_sem=all_sent, recv_sem=all_came,
        device_id=sibling, device_id_type=pl.DeviceIdType.MESH).wait_send()


def on_device(sections, reps, features, tiles, columns, weight):
    along, across = sections // 2, reps // 2
    side, width = features.shape
    arriving = len(arrivals(along, across))
    return pl.pallas_call(
        functools.partial(kernel, along, across),
        out_shape=pltpu.VMEM((side, weight.shape[1]), jnp.bfloat16),
        in_specs=[pl.BlockSpec(memory_space=pltpu.HBM)] * 4,
        out_specs=pl.BlockSpec(memory_space=pltpu.VMEM),
        scratch_shapes=[
            pltpu.VMEM((sections * reps, side, width), features.dtype),
            pltpu.VMEM(tiles.shape, tiles.dtype),
            pltpu.VMEM(weight.shape, weight.dtype),
            pltpu.SMEM(columns.shape, columns.dtype),
            pltpu.SemaphoreType.DMA((arriving,)),
            pltpu.SemaphoreType.DMA((arriving,)),
            pltpu.SemaphoreType.DMA,
            pltpu.SemaphoreType.DMA,
            pltpu.SemaphoreType.DMA((4,)),
        ],
        compiler_params=pltpu.CompilerParams(
            collective_id=0, has_side_effects=True, vmem_limit_bytes=56 * 1024 * 1024),
        cost_estimate=pl.CostEstimate(
            flops=2 * tiles.size * width, bytes_accessed=2 * (tiles.size + features.size * sections * reps),
            transcendentals=0),
    )(columns, features, tiles, weight)

def solution(mesh):
    return jax.shard_map(
        functools.partial(on_device, mesh.shape["section"], mesh.shape["rep"]),
        mesh=mesh,
        in_specs=(
            P(("section", "rep"), None),
            P(("section", "rep"), None, None, None),
            P(("section", "rep"), None),
            P(),
        ),
        out_specs=P(("section", "rep"), None),
        check_vma=False,
    )
```

```python
import functools
import jax
import jax.numpy as jnp
from jax import lax
from jax.experimental import pallas as pl
from jax.experimental.pallas import tpu as pltpu
from jax.sharding import PartitionSpec as P

GROUP = 8

def flip(index, wanted):
    return index + wanted - 2 * wanted * (index % 2)

def steps_of(columns):
    return [(0, 0)] + [(side, s) for s in range(1, columns) for side in (-1, 1)]

def arrivals(columns, across):
    keys = []
    for item in steps_of(columns):
        if item[1]:
            keys.append(("column", item))
        keys.append(("beside", item))
        for q in range(1, across):
            keys.append(("across", item, q))
            keys.extend(("diagonal", item, q, h) for h in range(3))
    return {key: spot for spot, key in enumerate(keys)}


def kernel(columns, across, c_ref, f_ref, t_ref, w_ref, out_ref, blocks, tiles, weight, col_ref, send_sems, recv_sems, all_sent, all_came, local_sems):
    rep = 2 * across
    side_rows = blocks.shape[1]
    half = side_rows // 2
    section_at = lax.axis_index("section")
    rep_at = lax.axis_index("rep")
    a, b = section_at // 2, section_at % 2
    x, c = rep_at // 2, rep_at % 2
    spots = arrivals(columns, across)
    climbed = []

    def device(item, beside, q, other):
        at = lax.rem(x + q, across) if q else x
        return (a + item[0] * item[1]) * 2 + flip(b, beside), at * 2 + flip(c, other)

    here = (0, 0)

    def block(item, beside, q, other=0):
        s, r = device(item, beside, q, other)
        return blocks.at[s * rep + r]

    def direct(item):
        return item[1] != 1

    def pieces(item):
        return (0,) if direct(item) else (1, 2)

    def part(ref, h):
        if h == 0:
            return ref
        h = h - 1
        return ref.at[pl.ds(h * half, half)]

    def there(item):
        if item[1] == 0:
            return None
        return a >= item[1] if item[0] < 0 else a + item[1] < columns

    def only(condition, work):
        if condition is None:
            work()
        else:
            pl.when(condition)(work)

    def send(src, dst, to, key):
        copy = pltpu.make_async_remote_copy(
            src_ref=src, dst_ref=dst, send_sem=send_sems.at[spots[key]] if key[0] == "column" else all_sent,
            recv_sem=all_came if key[0] == "sibling" else recv_sems.at[spots[key]],
            device_id=to, device_id_type=pl.DeviceIdType.MESH)
        copy.start()

    def arrive(dst, key):
        pltpu.make_async_remote_copy(
            src_ref=dst, dst_ref=dst, send_sem=send_sems.at[0], recv_sem=recv_sems.at[spots[key]],
            device_id=device(here, 0, 0, 1), device_id_type=pl.DeviceIdType.MESH).wait_recv()

    def gone(rows, key):
        src = blocks.at[0, pl.ds(0, rows)]
        pltpu.make_async_remote_copy(
            src_ref=src, dst_ref=src, send_sem=send_sems.at[spots[key]], recv_sem=recv_sems.at[spots[key]],
            device_id=device(here, 0, 0, 1), device_id_type=pl.DeviceIdType.MESH).wait_send()

    sibling = device(here, 0, 0, 1)
    beside = device(here, 1, 0, 0)

    barrier = pltpu.get_barrier_semaphore()

    def greet(partner):
        pl.semaphore_signal(barrier, inc=1, device_id=partner, device_id_type=pl.DeviceIdType.MESH)

    partners = [device(here, 0, q, 0) for q in range(1, across)] + [beside, sibling]
    partners += [device(here, 1, q, 0) for q in range(1, across)]
    partners += [(lax.rem(a + d, columns) * 2 + b, rep_at) for d in range(1, columns)]
    for partner in partners:
        greet(partner)
    pl.semaphore_wait(barrier, len(partners))

    def climb(s):
        for side, condition in ((-1, a + s < columns), (1, a >= s)):
            to, key = device((-side, s), 0, 0, 0), ("column", (side, s))
            only(condition, functools.partial(send, f_ref, block(here, 0, 0), to, key))
            climbed.append((s, key, condition))

    def wait_climb(s):
        for distance, key, condition in climbed:
            if distance == s:
                only(condition, functools.partial(gone, f_ref.shape[0], key))

    def pass_on(src, item):
        on = a + 1 < columns if item[0] < 0 else a >= 1
        to, key = device((-item[0], 1), 0, 0, 0), ("column", (item[0], 2))
        only(on, lambda: send(src, src, to, key))

    def spread(src, item):
        dst = block(item, 0, 0)
        for q in range(1, across):
            send(src, dst, device(here, 0, q, 0), ("across", item, q))
        send(src, dst, beside, ("beside", item))
        if direct(item):
            for q in range(1, across):
                send(src, dst, device(here, 1, q, 0), ("diagonal", item, q, 0))
        send(src, dst, sibling, ("sibling",))

    def receive(item):
        got = block(item, 0, 0)
        arrive(got, ("column", item))
        if item[1] == 1 and columns > 2:
            pass_on(got, item)
        spread(got, item)

    def relay(item):
        for q in range(1, across):
            got = block(item, 0, across - q)
            arrive(got, ("across", item, q))
            if not direct(item):
                send(part(got, 1), part(got, 1), beside, ("diagonal", item, q, 1))
            send(got, got, sibling, ("sibling",))
        got = block(item, 1, 0)
        arrive(got, ("beside", item))
        for q in range(1, across):
            if not direct(item):
                send(part(got, 2), part(got, 2), device(here, 0, q, 0), ("diagonal", item, q, 2))
        send(got, got, sibling, ("sibling",))

    def diagonal(item):
        for q in range(1, across):
            for h in pieces(item):
                got = part(block(item, 1, across - q), h)
                arrive(got, ("diagonal", item, q, h))
                send(got, got, sibling, ("sibling",))

    if columns > 1:
        climb(1)
    spread(f_ref, here)
    own = pltpu.make_async_copy(f_ref, block(here, 0, 0), local_sems.at[0])
    load_tiles = pltpu.make_async_copy(t_ref, tiles, local_sems.at[1])
    load_weight = pltpu.make_async_copy(w_ref, weight, local_sems.at[2])
    load_columns = pltpu.make_async_copy(c_ref, col_ref, local_sems.at[3])
    own.start()
    load_columns.start()
    load_tiles.start()
    load_weight.start()

    for s in range(3, columns):
        wait_climb(1 if s == 3 else s - 1)
        climb(s)

    rounds = [[here]] + [[(-1, s), (1, s)] for s in range(1, columns)]
    for s in range(len(rounds) + 2):
        for stage, at in ((receive, s), (relay, s - 1), (diagonal, s - 2)):
            if 0 <= at < len(rounds) and not (stage is receive and at == 0):
                for item in rounds[at]:
                    only(there(item), functools.partial(stage, item))
    whole = blocks.at[pl.ds(0, columns * 2 * across)]
    pltpu.make_async_remote_copy(
        src_ref=whole, dst_ref=whole, send_sem=all_sent, recv_sem=all_came,
        device_id=sibling, device_id_type=pl.DeviceIdType.MESH).wait_recv()
    own.wait()
    load_columns.wait()
    load_tiles.wait()
    load_weight.wait()

    number = tiles.shape[1]
    group = GROUP if number % GROUP == 0 else 1

    def step(i, total):
        left = jnp.concatenate([tiles[0, i * group + g] for g in range(group)], axis=1)
        right = jnp.concatenate([blocks[col_ref[0, i * group + g]] for g in range(group)], axis=0)
        return total + jnp.dot(left, right, preferred_element_type=jnp.float32)

    total = lax.fori_loop(0, number // group, step, jnp.zeros(out_ref.shape, jnp.float32), unroll=True)
    aggregated = total.astype(jnp.bfloat16)
    product = jnp.dot(aggregated, weight[...], preferred_element_type=jnp.float32)
    out_ref[...] = jnp.maximum(product, 0.0).astype(out_ref.dtype)

    if columns > 1:
        wait_climb(columns - 1 if columns > 3 else 1)
    if columns > 2:
        for item, condition in (((-1, 2), (a >= 1) & (a + 1 < columns)), ((1, 2), (a >= 1) & (a + 1 < columns))):
            only(condition, functools.partial(gone, f_ref.shape[0], ("column", item)))
    whole = blocks.at[pl.ds(0, columns * (4 * across - 1))]
    pltpu.make_async_remote_copy(
        src_ref=whole, dst_ref=whole, send_sem=all_sent, recv_sem=all_came,
        device_id=sibling, device_id_type=pl.DeviceIdType.MESH).wait_send()


def on_device(sections, reps, features, tiles, columns, weight):
    along, across = sections // 2, reps // 2
    side, width = features.shape
    arriving = len(arrivals(along, across))
    return pl.pallas_call(
        functools.partial(kernel, along, across),
        out_shape=pltpu.VMEM((side, weight.shape[1]), jnp.bfloat16),
        in_specs=[pl.BlockSpec(memory_space=pltpu.HBM)] * 4,
        out_specs=pl.BlockSpec(memory_space=pltpu.VMEM),
        scratch_shapes=[
            pltpu.VMEM((sections * reps, side, width), features.dtype),
            pltpu.VMEM(tiles.shape, tiles.dtype),
            pltpu.VMEM(weight.shape, weight.dtype),
            pltpu.SMEM(columns.shape, columns.dtype),
            pltpu.SemaphoreType.DMA((arriving,)),
            pltpu.SemaphoreType.DMA((arriving,)),
            pltpu.SemaphoreType.DMA,
            pltpu.SemaphoreType.DMA,
            pltpu.SemaphoreType.DMA((4,)),
        ],
        compiler_params=pltpu.CompilerParams(
            collective_id=0, has_side_effects=True, vmem_limit_bytes=56 * 1024 * 1024),
        cost_estimate=pl.CostEstimate(
            flops=2 * tiles.size * width, bytes_accessed=2 * (tiles.size + features.size * sections * reps),
            transcendentals=0),
    )(columns, features, tiles, weight)

def solution(mesh):
    return jax.shard_map(
        functools.partial(on_device, mesh.shape["section"], mesh.shape["rep"]),
        mesh=mesh,
        in_specs=(
            P(("section", "rep"), None),
            P(("section", "rep"), None, None, None),
            P(("section", "rep"), None),
            P(),
        ),
        out_specs=P(("section", "rep"), None),
        check_vma=False,
    )
```
